128 devices in a mesh: dp: 16 (over x, y_lo, core), tensor: 8 (over z, y_hi).
Axes of the slice: x: 4, y: 4 (y_hi: 2, y_lo: 2; y = y_hi * 2 + y_lo), z: 4, core: 2. Of those that a mesh axis runs over, the one named last changes fastest.
Arguments:
- gate_pre: bfloat16 [6144, 14336], P('dp', 'tensor'), may hold values from -6 to 6
- up_pre: bfloat16 [6144, 14336], P('dp', 'tensor'), may hold values from -6 to 6
- out_grad: bfloat16 [6144, 4096], P('dp'), may hold values from -6 to 6
- old_weight: float32 [14336, 4096], P(('dp', 'tensor')), may hold values from -0.046875 to 0.046875
- old_first: float32 [14336, 4096], P(('dp', 'tensor')), may hold values from -8 to 8
- old_second: float32 [14336, 4096], P(('dp', 'tensor')), may hold values from 1 to 1000
Outputs:
- new_weight: float32 [14336, 4096], P('tensor', 'dp')
- new_first: float32 [14336, 4096], P('tensor', 'dp')
- new_second: float32 [14336, 4096], P('tensor', 'dp')
- grad_gate: bfloat16 [6144, 14336], P('dp', 'tensor')
- grad_up: bfloat16 [6144, 14336], P('dp', 'tensor')
The draws below stay inside these ranges and needn't reach their ends.
All inputs are finite; a program needn't handle non-finite values.
Results may differ from the reference program's by a relative error of at most 0.0051.
Values may be sent and summed in bfloat16 or wider, within the bound.
A program may use at most 256 MiB of HBM per device.

```python
import math
import jax
import jax.numpy as jnp
from jax import lax

D = 4096
FF = 14336
TOK_DEV = 384
TOKENS = 6144
N_DP = 16


def raised(values, own_key, source, target, blocks, factor):
    def block_of(dim):
        return (jnp.arange(values.shape[dim]) // (values.shape[dim] // blocks)).reshape((-1,) + (1,) * (values.ndim - 1 - dim))

    first = jax.random.permutation(own_key, blocks)[block_of(target)]
    far = (block_of(target) + blocks // 2) % blocks
    return jnp.where((block_of(source) == first) | (block_of(source) == far), factor * values, values)


def steps_of(stream_key, extent, shards, low, high):
    def one(position, parts):
        steps = jax.random.uniform(jax.random.fold_in(jax.random.fold_in(stream_key, 6), position), (parts,), jnp.float32, low / len(shards), high / len(shards))
        return jnp.repeat(jnp.exp(steps), extent[position] // parts).reshape((-1,) + (1,) * (len(extent) - position - 1))

    loudness = one(*shards[0])
    for cut in shards[1:]:
        loudness = loudness * one(*cut)
    return loudness


def noise(key, shape, spread, bound, shards=(), kind=jnp.bfloat16):
    entries = spread * jax.random.normal(key, shape, jnp.float32)
    if shards:
        entries = entries * steps_of(key, shape, shards, -0.22, 0.18)
    return jnp.clip(entries, -bound, bound).astype(kind)


def bell_draw_with(key, shape, width, most, shards, heavy, held_as=jnp.bfloat16):
    drawn = width * jax.random.normal(key, shape, jnp.float32)
    if shards:
        drawn = drawn * steps_of(key, shape, shards, -0.22, 0.18)
    return jnp.clip(raised(drawn, jax.random.fold_in(key, 3), *heavy), -most, most).astype(held_as)


def setup_inputs(seed: int = 0) -> dict:
    streams_of = jax.random.split(jax.random.key(seed), 7)
    return {
        "gate_pre": noise(streams_of[0], (TOKENS, FF), 1.0, 6.0, ((0, 16), (1, 8))),
        "up_pre": noise(streams_of[1], (TOKENS, FF), 1.0, 6.0, ((0, 16), (1, 8))),
        "out_grad": bell_draw_with(streams_of[2], (TOKENS, D), 1.0, 6.0, ((0, 16),), (0, 1, 16, 2.0)),
        "old_weight": noise(streams_of[3], (FF, D), FF ** -0.5, 0.046875, ((0, 128),), jnp.float32),
        "old_first": noise(streams_of[4], (FF, D), 2.0, 8.0, ((0, 128),), jnp.float32),
        "old_second": jnp.clip(jnp.exp(math.log(1000.0) - 6.9077553 * jax.random.uniform(streams_of[5], (FF, D), jnp.float32) ** steps_of(streams_of[5], (FF, D), ((0, 128),), -0.2, 0.2)), 1.0, 1000.0),
    }


beta_one = 0.9
beta_two = 0.95
learn_rate = 0.0003
decay_rate = 0.1
epsilon = 1e-08
step_count = 1001

def adamw(weight, first, second, grad):
    first_new = beta_one * first + (1.0 - beta_one) * grad
    second_new = beta_two * second + (1.0 - beta_two) * grad * grad
    first_hat = first_new / (1.0 - beta_one ** step_count)
    second_hat = second_new / (1.0 - beta_two ** step_count)
    weight_new = weight - learn_rate * (first_hat / (jnp.sqrt(second_hat) + epsilon) + decay_rate * weight)
    return (weight_new, first_new, second_new)

def reference(gate_pre, up_pre, out_grad, old_weight, old_first, old_second):
    gate_f = gate_pre.astype(jnp.float32)
    up_f = up_pre.astype(jnp.float32)
    sig = jax.nn.sigmoid(gate_f)
    hidden = (gate_f * sig * up_f).astype(jnp.bfloat16)
    weight_half = old_weight.astype(jnp.bfloat16)
    hidden_grad = jnp.dot(out_grad, weight_half.T, preferred_element_type=jnp.float32)
    grad_gate = (hidden_grad * up_f * sig * (1.0 + gate_f * (1.0 - sig))).astype(jnp.bfloat16)
    grad_up = (hidden_grad * gate_f * sig).astype(jnp.bfloat16)
    hidden_parts = hidden.reshape(N_DP, TOK_DEV, FF)
    grad_parts = out_grad.reshape(N_DP, TOK_DEV, D)

    def add_block(running, pair):
        partial_grad = jnp.dot(pair[0].T, pair[1], preferred_element_type=jnp.float32)
        rounded = lax.optimization_barrier(partial_grad.astype(jnp.bfloat16)).astype(jnp.float32)
        return (running + rounded, None)
    weight_grad, unused = lax.scan(add_block, jnp.zeros((FF, D), jnp.float32), (hidden_parts, grad_parts))
    new_weight, new_first, new_second = adamw(old_weight, old_first, old_second, weight_grad)
    return (new_weight, new_first, new_second, grad_gate, grad_up)
```

```python
import functools
import jax
import jax.numpy as jnp
from jax import lax
from jax.experimental import pallas as pl
from jax.experimental.pallas import tpu as pltpu
from jax.sharding import PartitionSpec as P

beta_one = 0.9
beta_two = 0.95
learn_rate = 0.0003
decay_rate = 0.1
epsilon = 1e-08
step_count = 1001

MESH = pl.DeviceIdType.MESH
BF16 = jnp.bfloat16
F32 = jnp.float32


def adamw(weight, first, second, grad):
    first_new = beta_one * first + (1.0 - beta_one) * grad
    second_new = beta_two * second + (1.0 - beta_two) * grad * grad
    first_hat = first_new / (1.0 - beta_one**step_count)
    second_hat = second_new / (1.0 - beta_two**step_count)
    weight_new = weight - learn_rate * (
        first_hat / (jnp.sqrt(second_hat) + epsilon) + decay_rate * weight
    )
    return (weight_new, first_new, second_new)


def device(x, yl, c, z, yh):
    return ((x * 2 + yl) * 2 + c, z * 2 + yh)


def kernel(
    gate_hbm, up_hbm, og_hbm, w_hbm, m_hbm, v_hbm,
    gg_hbm, gu_hbm, grad_out, mv_out, wt_out,
    gate, up, w32, m32, v32, wb, mvb, og_all, h_own, h_all, w_all,
    part, rs, summed, hg, hg_all, gg, gu,
    load_sem, store_sem,
    ogy_s, ogy_r, ogz_s, ogz_r, ogc_s, ogc_r, h_s, h_r, w_s, w_r, mv_s, mv_r,
    hg_s, hg_r, wt_s, wt_r, rs_s, rs_r, g_s, g_r,
):
    d = lax.axis_index("dp")
    q = lax.axis_index("tensor")
    p = d // 2
    c = lax.rem(d, 2)
    x = p // 2
    yl = lax.rem(p, 2)
    z = q // 2
    yh = lax.rem(q, 2)
    tok, ff = gate.shape
    blk = w32.shape[0]
    cols = w32.shape[1]
    sub = cols // 16
    rows = 4 * blk
    tq = tok // 4
    mine = 2 * c + yl
    diag = p == q
    diag_i = jnp.where(diag, 1, 0)

    def mult(v, n):
        return pl.multiple_of(v, n)

    def peer(r):
        pyl = lax.rem(yl + r % 2, 2)
        pc = lax.rem(c + r // 2, 2)
        return device(x, pyl, pc, z, yh), 2 * pc + pyl, 2 * pyl + pc

    def across(r):
        return lax.rem(x + r, 4)

    loads = [
        pltpu.make_async_copy(og_hbm, og_all.at[pl.ds(mult(mine * tok, tok), tok)], load_sem.at[0]),
        pltpu.make_async_copy(w_hbm, w32, load_sem.at[1]),
        pltpu.make_async_copy(gate_hbm, gate, load_sem.at[2]),
        pltpu.make_async_copy(up_hbm, up, load_sem.at[3]),
        pltpu.make_async_copy(m_hbm, m32, load_sem.at[4]),
        pltpu.make_async_copy(v_hbm, v32, load_sem.at[5]),
    ]
    for load in loads:
        load.start()

    barrier = pltpu.get_barrier_semaphore()

    @pl.loop(0, 16)
    def _(n):
        @pl.when(jnp.logical_not(jnp.logical_and(diag, n == d)))
        def _():
            pl.semaphore_signal(barrier, inc=1, device_id=(n, p), device_id_type=MESH)

        sd = 2 * q + n // 8
        st = lax.rem(n, 8)

        @pl.when(jnp.logical_not(jnp.logical_and(sd == d, st == q)))
        def _():
            pl.semaphore_signal(barrier, inc=1, device_id=(sd, st), device_id_type=MESH)

    for r in range(1, 4):
        pl.semaphore_signal(barrier, inc=1, device_id=peer(r)[0], device_id_type=MESH)
        pl.semaphore_signal(
            barrier, inc=1, device_id=device(across(r), yl, c, z, yh), device_id_type=MESH
        )
        pl.semaphore_signal(
            barrier, inc=1, device_id=device(x, yl, c, lax.rem(z + r, 4), yh), device_id_type=MESH
        )

    loads[1].wait()
    wb[...] = w32[...].astype(BF16)
    loads[0].wait()
    pl.semaphore_wait(barrier, 41 - 2 * diag_i)

    def remote(src, dst, ss, rr, to):
        return pltpu.make_async_remote_copy(
            src_ref=src, dst_ref=dst, send_sem=ss, recv_sem=rr, device_id=to, device_id_type=MESH
        )

    sends = []

    def go(*args):
        copy = remote(*args)
        copy.start()
        sends.append(copy)

    def og_rows(slot, part_index):
        return og_all.at[pl.ds(mult(slot * tok + part_index * tq, tq), tq)]

    def og_slot(slot):
        return og_all.at[pl.ds(mult(slot * tok, tok), tok)]

    side, side_slot, _ = peer(1)
    core, core_slot, _ = peer(2)
    _, far_slot, _ = peer(3)
    go(og_rows(mine, z), og_rows(mine, z), ogy_s, ogy_r, side)
    go(og_slot(mine), og_slot(mine), ogc_s.at[4], ogc_r.at[4], core)

    block = 2 * lax.rem(z, 2) + yh
    w_dst = w_all.at[pl.ds(mult(block * blk, blk), blk)]
    w_yl = z // 2
    self_w = jnp.logical_and(diag, w_yl == yl)
    for r in range(1, 4):
        go(wb, w_dst, w_s.at[r], w_r.at[block], device(across(r), w_yl, c, x, yl))
    w_home = remote(wb, w_dst, w_s.at[0], w_r.at[block], device(x, w_yl, c, x, yl))

    @pl.when(self_w)
    def _():
        pltpu.make_async_copy(wb, w_dst, w_r.at[block]).start()

    @pl.when(jnp.logical_not(self_w))
    def _():
        w_home.start()

    loads[4].wait()
    loads[5].wait()
    for n in range(16):
        mvb[n, 0] = m32[:, n * sub : (n + 1) * sub].astype(BF16)
        mvb[n, 1] = v32[:, n * sub : (n + 1) * sub].astype(BF16)
    mv_dst = mv_out.at[:, pl.ds(mult((8 * c + q) * blk, blk), blk), :]

    @pl.when(diag)
    def _():
        pltpu.make_async_copy(mvb.at[d], mv_dst, mv_r).start()

    @pl.when(jnp.logical_not(diag))
    def _():
        remote(mvb.at[d], mv_dst, mv_s.at[0], mv_r, (d, p)).start()

    @pl.loop(1, 16)
    def _(r):
        n = lax.rem(d + r, 16)
        remote(mvb.at[n], mv_dst, mv_s.at[r], mv_r, (n, p)).start()

    loads[2].wait()
    loads[3].wait()

    @pl.loop(0, ff // 128)
    def _(b):
        at = pl.ds(mult(b * 128, 128), 128)
        g = gate[:, at].astype(F32)
        u = up[:, at].astype(F32)
        h = g * jax.nn.sigmoid(g) * u
        h_own[at, :] = h.T.astype(BF16)

    my_cols = pl.ds(mult(mine * tok, 128), tok)
    for r in range(1, 4):
        to, slot, _ = peer(r)
        go(h_own.at[pl.ds(mult(slot * rows, rows), rows)], h_all.at[:, my_cols],
           h_s.at[r - 1], h_r.at[r - 1], to)
    h_all[:, my_cols] = h_own[pl.ds(mult(mine * rows, rows), rows), :]

    got = og_rows(side_slot, z)
    remote(got, got, ogy_s, ogy_r, side).wait_recv()
    for r in range(1, 4):
        go(got, got, ogz_s.at[r - 1], ogz_r.at[r - 1], device(x, yl, c, lax.rem(z + r, 4), yh))
    go(got, got, ogc_s.at[0], ogc_r.at[0], core)
    for r in (1, 3, 2):
        got = og_rows(side_slot, lax.rem(z + 4 - r, 4))
        remote(got, got, ogz_s.at[r - 1], ogz_r.at[r - 1], side).wait_recv()
        go(got, got, ogc_s.at[r], ogc_r.at[r], core)

    for r in range(1, 4):
        _, slot, _ = peer(r)
        there = h_all.at[:, pl.ds(mult(slot * tok, 128), tok)]
        remote(there, there, h_s.at[r - 1], h_r.at[r - 1], side).wait_recv()
    remote(og_slot(core_slot), og_slot(core_slot), ogc_s.at[4], ogc_r.at[4], core).wait_recv()
    for r in range(4):
        got = og_rows(far_slot, lax.rem(z + 4 - r, 4))
        remote(got, got, ogc_s.at[r], ogc_r.at[r], core).wait_recv()

    @pl.loop(0, 4)
    def _(k):
        for r in (1, 3, 2, 0):
            to_x = across(r)
            at = pl.ds(mult((to_x * 4 + k) * sub, 128), sub)
            part[r, k] = jnp.dot(
                h_all[...], og_all[:, at], preferred_element_type=F32
            ).astype(BF16)
            if r:
                remote(part.at[r, k], rs.at[r - 1, k], rs_s.at[r - 1, k], rs_r.at[r - 1, k],
                       device(to_x, yl, c, z, yh)).start()

    for i in range(4):
        there = w_all.at[pl.ds(i * blk, blk)]
        remote(there, there, w_s.at[0], w_r.at[i], side).wait_recv()
    my_rows = pl.ds(mult(mine * rows, rows), rows)
    for r in range(1, 4):
        to, _, k = peer(r)
        go(w_all.at[:, pl.ds(mult((x * 4 + k) * sub, 128), sub)], wt_out.at[my_rows],
           wt_s.at[r - 1], wt_r.at[r - 1], to)
    wt_own = pltpu.make_async_copy(
        w_all.at[:, pl.ds(mult(d * sub, 128), sub)], wt_out.at[my_rows], store_sem.at[0]
    )
    wt_own.start()

    n_tile = 4 * tok // 6

    @pl.loop(0, 6)
    def _(n):
        at = pl.ds(mult(n * n_tile, n_tile), n_tile)
        hg[:, at] = lax.dot_general(
            w_all[...], og_all[at, :], (((1,), (1,)), ((), ())), preferred_element_type=F32
        ).astype(BF16)

    for r in range(1, 4):
        to, slot, _ = peer(r)
        go(hg.at[:, pl.ds(mult(slot * tok, 128), tok)], hg_all.at[my_rows],
           hg_s.at[r - 1], hg_r.at[r - 1], to)
    hg_all[my_rows, :] = hg[:, my_cols]

    def reduce_chunk(k):
        for r in range(3):
            remote(rs.at[r, k], rs.at[r, k], rs_s.at[r, k], rs_r.at[r, k], side).wait_recv()
        summed[k] = (
            part[0, k].astype(F32) + rs[0, k].astype(F32)
            + (rs[1, k].astype(F32) + rs[2, k].astype(F32))
        ).astype(BF16)
        k_yl = k // 2
        k_c = k % 2
        r = (1 - jnp.where(k_yl == yl, 1, 0)) + 2 * (1 - jnp.where(k_c == c, 1, 0))
        local = r == 0
        dst = grad_out.at[my_rows]

        @pl.when(local)
        def _():
            pltpu.make_async_copy(summed.at[k], dst, store_sem.at[1]).start()

        @pl.when(jnp.logical_not(local))
        def _():
            remote(summed.at[k], dst, g_s.at[r], g_r.at[r], device(x, k_yl, k_c, z, yh)).start()

    def finish_grads():
        for r in range(1, 4):
            _, slot, _ = peer(r)
            there = hg_all.at[pl.ds(mult(slot * rows, rows), rows)]
            remote(there, there, hg_s.at[r - 1], hg_r.at[r - 1], side).wait_recv()

        @pl.loop(0, ff // 128)
        def _(b):
            at = pl.ds(mult(b * 128, 128), 128)
            back = hg_all[at, :].astype(F32).T
            g = gate[:, at].astype(F32)
            u = up[:, at].astype(F32)
            s = jax.nn.sigmoid(g)
            gg[:, at] = (back * u * s * (1.0 + g * (1.0 - s))).astype(BF16)
            gu[:, at] = (back * g * s).astype(BF16)

        pltpu.make_async_copy(gg, gg_hbm, store_sem.at[2]).start()
        pltpu.make_async_copy(gu, gu_hbm, store_sem.at[3]).start()

    for k in range(4):
        if k == 3:
            finish_grads()
        reduce_chunk(k)

    for copy in sends:
        copy.wait_send()

    @pl.when(jnp.logical_not(self_w))
    def _():
        w_home.wait_send()

    @pl.when(jnp.logical_not(diag))
    def _():
        remote(mvb.at[0], mv_dst, mv_s.at[0], mv_r, side).wait_send()

    for r in range(1, 16):
        remote(mvb.at[r], mv_dst, mv_s.at[r], mv_r, side).wait_send()
    for r in range(3):
        for k in range(4):
            remote(part.at[r + 1, k], rs.at[r, k], rs_s.at[r, k], rs_r.at[r, k], side).wait_send()
    pltpu.make_async_copy(gg, gg_hbm, store_sem.at[2]).wait()
    pltpu.make_async_copy(gu, gu_hbm, store_sem.at[3]).wait()
    wt_own.wait()
    pltpu.make_async_copy(summed.at[0], grad_out.at[my_rows], store_sem.at[1]).wait()
    for r in range(1, 4):
        _, slot, _ = peer(r)
        there = pl.ds(mult(slot * rows, rows), rows)
        remote(wt_out.at[there], wt_out.at[there], wt_s.at[r - 1], wt_r.at[r - 1], side).wait_recv()
        remote(summed.at[r], grad_out.at[there], g_s.at[r], g_r.at[r], side).wait()
    remote(mv_out, mv_out, mv_s.at[0], mv_r, side).wait_recv()


def body(gate_pre, up_pre, out_grad, old_weight, old_first, old_second):
    tok, ff = gate_pre.shape
    blk, cols = old_weight.shape
    rows = 4 * blk
    sub = cols // 16
    anyspec = pl.BlockSpec(memory_space=pl.ANY)
    dma = pltpu.SemaphoreType.DMA
    gg, gu, grad, moments, weight = pl.pallas_call(
        kernel,
        out_shape=(
            jax.ShapeDtypeStruct((tok, ff), BF16),
            jax.ShapeDtypeStruct((tok, ff), BF16),
            jax.ShapeDtypeStruct((ff, sub), BF16),
            jax.ShapeDtypeStruct((2, ff, sub), BF16),
            jax.ShapeDtypeStruct((ff, sub), BF16),
        ),
        in_specs=[anyspec] * 6,
        out_specs=(anyspec,) * 5,
        scratch_shapes=[
            pltpu.VMEM((tok, ff), BF16),
            pltpu.VMEM((tok, ff), BF16),
            pltpu.VMEM((blk, cols), F32),
            pltpu.VMEM((blk, cols), F32),
            pltpu.VMEM((blk, cols), F32),
            pltpu.VMEM((blk, cols), BF16),
            pltpu.VMEM((16, 2, blk, sub), BF16),
            pltpu.VMEM((4 * tok, cols), BF16),
            pltpu.VMEM((ff, tok), BF16),
            pltpu.VMEM((rows, 4 * tok), BF16),
            pltpu.VMEM((rows, cols), BF16),
            pltpu.VMEM((4, 4, rows, sub), BF16),
            pltpu.VMEM((3, 4, rows, sub), BF16),
            pltpu.VMEM((4, rows, sub), BF16),
            pltpu.VMEM((rows, 4 * tok), BF16),
            pltpu.VMEM((ff, tok), BF16),
            pltpu.VMEM((tok, ff), BF16),
            pltpu.VMEM((tok, ff), BF16),
            dma((6,)),
            dma((4,)),
            dma(()), dma(()),
            dma((3,)), dma((3,)),
            dma((5,)), dma((5,)),
            dma((3,)), dma((3,)),
            dma((4,)), dma((4,)),
            dma((16,)), dma(()),
            dma((3,)), dma((3,)),
            dma((3,)), dma((3,)),
            dma((3, 4)), dma((3, 4)),
            dma((4,)), dma((4,)),
        ],
        compiler_params=pltpu.CompilerParams(
            collective_id=0, has_side_effects=True, vmem_limit_bytes=60 << 20
        ),
        cost_estimate=pl.CostEstimate(
            flops=4 * tok * ff * cols, bytes_accessed=6 * tok * ff * 2, transcendentals=2 * tok * ff
        ),
        name="step",
    )(gate_pre, up_pre, out_grad, old_weight, old_first, old_second)
    new_weight, new_first, new_second = adamw(
        weight.astype(F32), moments[0].astype(F32), moments[1].astype(F32), grad.astype(F32)
    )
    return (new_weight, new_first, new_second, gg, gu)


def solution(mesh):
    placed = (
        P("dp", "tensor"),
        P("dp", "tensor"),
        P("dp", None),
        P(("dp", "tensor"), None),
        P(("dp", "tensor"), None),
        P(("dp", "tensor"), None),
    )
    return jax.shard_map(
        body,
        mesh=mesh,
        in_specs=placed,
        out_specs=(
            P("tensor", "dp"),
            P("tensor", "dp"),
            P("tensor", "dp"),
            P("dp", "tensor"),
            P("dp", "tensor"),
        ),
        check_vma=False,
    )
```

```python
import functools
import jax
import jax.numpy as jnp
from jax import lax
from jax.experimental import pallas as pl
from jax.experimental.pallas import tpu as pltpu
from jax.sharding import PartitionSpec as P

beta_one = 0.9
beta_two = 0.95
learn_rate = 0.0003
decay_rate = 0.1
epsilon = 1e-08
step_count = 1001

MESH = pl.DeviceIdType.MESH
BF16 = jnp.bfloat16
F32 = jnp.float32


def adamw(weight, first, second, grad):
    first_new = beta_one * first + (1.0 - beta_one) * grad
    second_new = beta_two * second + (1.0 - beta_two) * grad * grad
    first_hat = first_new / (1.0 - beta_one**step_count)
    second_hat = second_new / (1.0 - beta_two**step_count)
    weight_new = weight - learn_rate * (
        first_hat / (jnp.sqrt(second_hat) + epsilon) + decay_rate * weight
    )
    return (weight_new, first_new, second_new)


def device(x, yl, c, z, yh):
    return ((x * 2 + yl) * 2 + c, z * 2 + yh)


def kernel(
    gate_hbm, up_hbm, og_hbm, w_hbm, m_hbm, v_hbm,
    gg_hbm, gu_hbm, grad_out, mv_out, wt_out,
    gate, up, w32, m32, v32, wb, mvb, og_all, h_own, h_all, w_all,
    part, rs, summed, hg, hg_all, gg, gu,
    load_sem, store_sem,
    ogy_s, ogy_r, ogz_s, ogz_r, ogc_s, ogc_r, h_s, h_r, w_s, w_r, wx_s, wx_r, mv_s, mv_r,
    hg_s, hg_r, wt_s, wt_r, rs_s, rs_r, g_s, g_r,
):
    d = lax.axis_index("dp")
    q = lax.axis_index("tensor")
    p = d // 2
    c = lax.rem(d, 2)
    x = p // 2
    yl = lax.rem(p, 2)
    z = q // 2
    yh = lax.rem(q, 2)
    tok, ff = gate.shape
    blk = w32.shape[0]
    cols = w32.shape[1]
    sub = cols // 16
    rows = 4 * blk
    tq = tok // 4
    mine = 2 * c + yl
    diag = p == q
    diag_i = jnp.where(diag, 1, 0)

    def mult(v, n):
        return pl.multiple_of(v, n)

    def peer(r):
        pyl = lax.rem(yl + r % 2, 2)
        pc = lax.rem(c + r // 2, 2)
        return device(x, pyl, pc, z, yh), 2 * pc + pyl, 2 * pyl + pc

    def across(r):
        return lax.rem(x + r, 4)

    loads = [
        pltpu.make_async_copy(og_hbm, og_all.at[pl.ds(mult(mine * tok, tok), tok)], load_sem.at[0]),
        pltpu.make_async_copy(w_hbm, w32, load_sem.at[1]),
        pltpu.make_async_copy(gate_hbm, gate, load_sem.at[2]),
        pltpu.make_async_copy(up_hbm, up, load_sem.at[3]),
        pltpu.make_async_copy(m_hbm, m32, load_sem.at[4]),
        pltpu.make_async_copy(v_hbm, v32, load_sem.at[5]),
    ]
    for load in loads:
        load.start()

    barrier = pltpu.get_barrier_semaphore()

    @pl.loop(0, 16)
    def _(n):
        @pl.when(jnp.logical_not(jnp.logical_and(diag, n == d)))
        def _():
            pl.semaphore_signal(barrier, inc=1, device_id=(n, p), device_id_type=MESH)

        sd = 2 * q + n // 8
        st = lax.rem(n, 8)

        @pl.when(jnp.logical_not(jnp.logical_and(sd == d, st == q)))
        def _():
            pl.semaphore_signal(barrier, inc=1, device_id=(sd, st), device_id_type=MESH)

    for r in range(1, 4):
        pl.semaphore_signal(barrier, inc=1, device_id=peer(r)[0], device_id_type=MESH)
        pl.semaphore_signal(
            barrier, inc=1, device_id=device(across(r), yl, c, z, yh), device_id_type=MESH
        )
        pl.semaphore_signal(
            barrier, inc=1, device_id=device(x, yl, c, lax.rem(z + r, 4), yh), device_id_type=MESH
        )

    loads[0].wait()
    loads[1].wait()
    for n in range(4):
        wb[n] = w32[:, n * 4 * sub : (n + 1) * 4 * sub].astype(BF16)
    pl.semaphore_wait(barrier, 41 - 2 * diag_i)

    def remote(src, dst, ss, rr, to):
        return pltpu.make_async_remote_copy(
            src_ref=src, dst_ref=dst, send_sem=ss, recv_sem=rr, device_id=to, device_id_type=MESH
        )

    sends = []

    def go(*args):
        copy = remote(*args)
        copy.start()
        sends.append(copy)

    half = tq // 2

    def og_half(slot, part_index, side_half):
        start = mult(slot * tok + part_index * tq + side_half * half, half)
        return og_all.at[pl.ds(start, half)]

    def og_slot(slot):
        return og_all.at[pl.ds(mult(slot * tok, tok), tok)]

    side, side_slot, _ = peer(1)
    core, core_slot, _ = peer(2)
    _, far_slot, _ = peer(3)
    for i in range(2):
        mine_half = og_half(mine, z, i)
        go(mine_half, mine_half, ogy_s.at[i], ogy_r.at[i], side)

    block = 2 * lax.rem(z, 2) + yh
    w_yl = z // 2
    self_w = jnp.logical_and(diag, w_yl == yl)

    def w_cols(at_x):
        return pl.ds(mult(at_x * 4 * sub, 128), 4 * sub)

    def w_place(at_x):
        return w_all.at[pl.ds(mult(block * blk, blk), blk), w_cols(at_x)]

    for r in (1, 3, 2):
        go(wb.at[across(r)], w_place(across(r)), w_s.at[r], w_r.at[block],
           device(across(r), w_yl, c, x, yl))
    w_home = remote(wb.at[x], w_place(x), w_s.at[0], w_r.at[block], device(x, w_yl, c, x, yl))

    @pl.when(self_w)
    def _():
        pltpu.make_async_copy(wb.at[x], w_place(x), w_r.at[block]).start()

    @pl.when(jnp.logical_not(self_w))
    def _():
        w_home.start()

    go(og_slot(mine), og_slot(mine), ogc_s.at[8], ogc_r.at[8], core)

    loads[4].wait()
    loads[5].wait()
    for n in range(16):
        mvb[n, 0] = m32[:, n * sub : (n + 1) * sub].astype(BF16)
        mvb[n, 1] = v32[:, n * sub : (n + 1) * sub].astype(BF16)
    mv_dst = mv_out.at[:, pl.ds(mult((8 * c + q) * blk, blk), blk), :]

    @pl.when(diag)
    def _():
        pltpu.make_async_copy(mvb.at[d], mv_dst, mv_r).start()

    @pl.when(jnp.logical_not(diag))
    def _():
        remote(mvb.at[d], mv_dst, mv_s.at[0], mv_r, (d, p)).start()

    @pl.loop(1, 16)
    def _(r):
        n = lax.rem(d + r, 16)
        remote(mvb.at[n], mv_dst, mv_s.at[r], mv_r, (n, p)).start()

    loads[2].wait()
    loads[3].wait()

    @pl.loop(0, ff // 128)
    def _(b):
        at = pl.ds(mult(b * 128, 128), 128)
        g = gate[:, at].astype(F32)
        u = up[:, at].astype(F32)
        h = g * jax.nn.sigmoid(g) * u
        h_own[at, :] = h.T.astype(BF16)

    my_cols = pl.ds(mult(mine * tok, 128), tok)
    for r in range(1, 4):
        to, slot, _ = peer(r)
        go(h_own.at[pl.ds(mult(slot * rows, rows), rows)], h_all.at[:, my_cols],
           h_s.at[r - 1], h_r.at[r - 1], to)
    h_all[:, my_cols] = h_own[pl.ds(mult(mine * rows, rows), rows), :]

    z_next = device(x, yl, c, lax.rem(z + 1, 4), yh)
    z_prev = device(x, yl, c, lax.rem(z + 3, 4), yh)
    x_next = device(across(1), yl, c, z, yh)
    x_prev = device(across(3), yl, c, z, yh)

    def quarter(r):
        return lax.rem(z + 4 - r, 4)

    def z_piece(i):
        return og_half(side_slot, quarter((1, 1, 3, 3, 2, 2)[i]), i % 2)

    def z_wait(i):
        got = z_piece(i)
        remote(got, got, ogz_s.at[i], ogz_r.at[i], z_next).wait_recv()
        if i == 0:
            go(got, got, ogz_s.at[4], ogz_r.at[4], z_next)
        if i == 3:
            go(got, got, ogz_s.at[5], ogz_r.at[5], z_prev)
        go(got, got, ogc_s.at[2 + i], ogc_r.at[2 + i], core)

    def y_wait(i):
        got = og_half(side_slot, z, i)
        remote(got, got, ogy_s.at[i], ogy_r.at[i], side).wait_recv()
        up_z = (got, got, ogz_s.at[i], ogz_r.at[i], z_next)
        down_z = (got, got, ogz_s.at[2 + i], ogz_r.at[2 + i], z_prev)
        for which in ((up_z, down_z), (down_z, up_z))[i]:
            go(*which)
        go(got, got, ogc_s.at[i], ogc_r.at[i], core)

    half_rows = rows // 2

    def w_half(at_x, i):
        return w_all.at[pl.ds(i * half_rows, half_rows), w_cols(at_x)]

    def wx_piece(i):
        return w_half(across((3, 3, 1, 1, 2, 2)[i]), i % 2)

    def wx_wait(i):
        got = wx_piece(i)
        remote(got, got, wx_s.at[i], wx_r.at[i], x_next).wait_recv()
        if i == 0:
            go(got, got, wx_s.at[4], wx_r.at[4], x_next)
        if i == 3:
            go(got, got, wx_s.at[5], wx_r.at[5], x_prev)

    y_wait(0)
    for i in range(4):
        there = w_all.at[pl.ds(i * blk, blk), w_cols(x)]
        remote(there, there, w_s.at[0], w_r.at[i], side).wait_recv()
    for i in range(2):
        got = w_half(x, i)
        mate = w_half(x, 1 - i)
        go(got, got, wx_s.at[i], wx_r.at[i], x_next)
        go(mate, mate, wx_s.at[3 - i], wx_r.at[3 - i], x_prev)
    y_wait(1)
    z_wait(0)
    z_wait(3)
    wx_wait(0)
    wx_wait(3)
    for i in (1, 2, 4, 5):
        z_wait(i)

    for r in range(1, 4):
        _, slot, _ = peer(r)
        there = h_all.at[:, pl.ds(mult(slot * tok, 128), tok)]
        remote(there, there, h_s.at[r - 1], h_r.at[r - 1], side).wait_recv()
    remote(og_slot(core_slot), og_slot(core_slot), ogc_s.at[8], ogc_r.at[8], core).wait_recv()
    for i in range(8):
        got = og_half(far_slot, quarter((0, 0, 1, 1, 3, 3, 2, 2)[i]), i % 2)
        remote(got, got, ogc_s.at[i], ogc_r.at[i], core).wait_recv()

    @pl.loop(0, 4)
    def _(k):
        for r in (1, 3, 2, 0):
            to_x = across(r)
            at = pl.ds(mult((to_x * 4 + k) * sub, 128), sub)
            part[r, k] = jnp.dot(
                h_all[...], og_all[:, at], preferred_element_type=F32
            ).astype(BF16)
            if r:
                remote(part.at[r, k], rs.at[r - 1, k], rs_s.at[r - 1, k], rs_r.at[r - 1, k],
                       device(to_x, yl, c, z, yh)).start()

    for i in (1, 2, 4, 5):
        wx_wait(i)
    my_rows = pl.ds(mult(mine * rows, rows), rows)
    for r in range(1, 4):
        to, _, k = peer(r)
        go(w_all.at[:, pl.ds(mult((x * 4 + k) * sub, 128), sub)], wt_out.at[my_rows],
           wt_s.at[r - 1], wt_r.at[r - 1], to)
    wt_own = pltpu.make_async_copy(
        w_all.at[:, pl.ds(mult(d * sub, 128), sub)], wt_out.at[my_rows], store_sem.at[0]
    )
    wt_own.start()

    n_tile = 4 * tok // 6

    @pl.loop(0, 6)
    def _(n):
        at = pl.ds(mult(n * n_tile, n_tile), n_tile)
        hg[:, at] = lax.dot_general(
            w_all[...], og_all[at, :], (((1,), (1,)), ((), ())), preferred_element_type=F32
        ).astype(BF16)

    for r in range(1, 4):
        to, slot, _ = peer(r)
        go(hg.at[:, pl.ds(mult(slot * tok, 128), tok)], hg_all.at[my_rows],
           hg_s.at[r - 1], hg_r.at[r - 1], to)
    hg_all[my_rows, :] = hg[:, my_cols]

    def reduce_chunk(k):
        for r in range(3):
            remote(rs.at[r, k], rs.at[r, k], rs_s.at[r, k], rs_r.at[r, k], side).wait_recv()
        summed[k] = (
            part[0, k].astype(F32) + rs[0, k].astype(F32)
            + (rs[1, k].astype(F32) + rs[2, k].astype(F32))
        ).astype(BF16)
        k_yl = k // 2
        k_c = k % 2
        r = (1 - jnp.where(k_yl == yl, 1, 0)) + 2 * (1 - jnp.where(k_c == c, 1, 0))
        local = r == 0
        dst = grad_out.at[my_rows]

        @pl.when(local)
        def _():
            pltpu.make_async_copy(summed.at[k], dst, store_sem.at[1]).start()

        @pl.when(jnp.logical_not(local))
        def _():
            remote(summed.at[k], dst, g_s.at[r], g_r.at[r], device(x, k_yl, k_c, z, yh)).start()

    def finish_grads():
        for r in range(1, 4):
            _, slot, _ = peer(r)
            there = hg_all.at[pl.ds(mult(slot * rows, rows), rows)]
            remote(there, there, hg_s.at[r - 1], hg_r.at[r - 1], side).wait_recv()

        @pl.loop(0, ff // 128)
        def _(b):
            at = pl.ds(mult(b * 128, 128), 128)
            back = hg_all[at, :].astype(F32).T
            g = gate[:, at].astype(F32)
            u = up[:, at].astype(F32)
            s = jax.nn.sigmoid(g)
            gg[:, at] = (back * u * s * (1.0 + g * (1.0 - s))).astype(BF16)
            gu[:, at] = (back * g * s).astype(BF16)

        pltpu.make_async_copy(gg, gg_hbm, store_sem.at[2]).start()
        pltpu.make_async_copy(gu, gu_hbm, store_sem.at[3]).start()

    for k in range(4):
        if k == 3:
            finish_grads()
        reduce_chunk(k)

    for copy in sends:
        copy.wait_send()

    @pl.when(jnp.logical_not(self_w))
    def _():
        w_home.wait_send()

    @pl.when(jnp.logical_not(diag))
    def _():
        remote(mvb.at[0], mv_dst, mv_s.at[0], mv_r, side).wait_send()

    for r in range(1, 16):
        remote(mvb.at[r], mv_dst, mv_s.at[r], mv_r, side).wait_send()
    for r in range(3):
        for k in range(4):
            remote(part.at[r + 1, k], rs.at[r, k], rs_s.at[r, k], rs_r.at[r, k], side).wait_send()
    pltpu.make_async_copy(gg, gg_hbm, store_sem.at[2]).wait()
    pltpu.make_async_copy(gu, gu_hbm, store_sem.at[3]).wait()
    wt_own.wait()
    pltpu.make_async_copy(summed.at[0], grad_out.at[my_rows], store_sem.at[1]).wait()
    for r in range(1, 4):
        _, slot, _ = peer(r)
        there = pl.ds(mult(slot * rows, rows), rows)
        remote(wt_out.at[there], wt_out.at[there], wt_s.at[r - 1], wt_r.at[r - 1], side).wait_recv()
        remote(summed.at[r], grad_out.at[there], g_s.at[r], g_r.at[r], side).wait()
    remote(mv_out, mv_out, mv_s.at[0], mv_r, side).wait_recv()


def body(gate_pre, up_pre, out_grad, old_weight, old_first, old_second):
    tok, ff = gate_pre.shape
    blk, cols = old_weight.shape
    rows = 4 * blk
    sub = cols // 16
    anyspec = pl.BlockSpec(memory_space=pl.ANY)
    dma = pltpu.SemaphoreType.DMA
    gg, gu, grad, moments, weight = pl.pallas_call(
        kernel,
        out_shape=(
            jax.ShapeDtypeStruct((tok, ff), BF16),
            jax.ShapeDtypeStruct((tok, ff), BF16),
            jax.ShapeDtypeStruct((ff, sub), BF16),
            jax.ShapeDtypeStruct((2, ff, sub), BF16),
            jax.ShapeDtypeStruct((ff, sub), BF16),
        ),
        in_specs=[anyspec] * 6,
        out_specs=(anyspec,) * 5,
        scratch_shapes=[
            pltpu.VMEM((tok, ff), BF16),
            pltpu.VMEM((tok, ff), BF16),
            pltpu.VMEM((blk, cols), F32),
            pltpu.VMEM((blk, cols), F32),
            pltpu.VMEM((blk, cols), F32),
            pltpu.VMEM((4, blk, cols // 4), BF16),
            pltpu.VMEM((16, 2, blk, sub), BF16),
            pltpu.VMEM((4 * tok, cols), BF16),
            pltpu.VMEM((ff, tok), BF16),
            pltpu.VMEM((rows, 4 * tok), BF16),
            pltpu.VMEM((rows, cols), BF16),
            pltpu.VMEM((4, 4, rows, sub), BF16),
            pltpu.VMEM((3, 4, rows, sub), BF16),
            pltpu.VMEM((4, rows, sub), BF16),
            pltpu.VMEM((rows, 4 * tok), BF16),
            pltpu.VMEM((ff, tok), BF16),
            pltpu.VMEM((tok, ff), BF16),
            pltpu.VMEM((tok, ff), BF16),
            dma((6,)),
            dma((4,)),
            dma((2,)), dma((2,)),
            dma((6,)), dma((6,)),
            dma((9,)), dma((9,)),
            dma((3,)), dma((3,)),
            dma((4,)), dma((4,)),
            dma((6,)), dma((6,)),
            dma((16,)), dma(()),
            dma((3,)), dma((3,)),
            dma((3,)), dma((3,)),
            dma((3, 4)), dma((3, 4)),
            dma((4,)), dma((4,)),
        ],
        compiler_params=pltpu.CompilerParams(
            collective_id=0, has_side_effects=True, vmem_limit_bytes=60 << 20
        ),
        cost_estimate=pl.CostEstimate(
            flops=4 * tok * ff * cols, bytes_accessed=6 * tok * ff * 2, transcendentals=2 * tok * ff
        ),
        name="step",
    )(gate_pre, up_pre, out_grad, old_weight, old_first, old_second)
    new_weight, new_first, new_second = adamw(
        weight.astype(F32), moments[0].astype(F32), moments[1].astype(F32), grad.astype(F32)
    )
    return (new_weight, new_first, new_second, gg, gu)


def solution(mesh):
    placed = (
        P("dp", "tensor"),
        P("dp", "tensor"),
        P("dp", None),
        P(("dp", "tensor"), None),
        P(("dp", "tensor"), None),
        P(("dp", "tensor"), None),
    )
    return jax.shard_map(
        body,
        mesh=mesh,
        in_specs=placed,
        out_specs=(
            P("tensor", "dp"),
            P("tensor", "dp"),
            P("tensor", "dp"),
            P("dp", "tensor"),
            P("dp", "tensor"),
        ),
        check_vma=False,
    )
```

```python
import functools
import jax
import jax.numpy as jnp
from jax import lax
from jax.experimental import pallas as pl
from jax.experimental.pallas import tpu as pltpu
from jax.sharding import PartitionSpec as P

beta_one = 0.9
beta_two = 0.95
learn_rate = 0.0003
decay_rate = 0.1
epsilon = 1e-08
step_count = 1001

MESH = pl.DeviceIdType.MESH
BF16 = jnp.bfloat16
F32 = jnp.float32


def adamw(weight, first, second, grad):
    first_new = beta_one * first + (1.0 - beta_one) * grad
    second_new = beta_two * second + (1.0 - beta_two) * grad * grad
    first_hat = first_new / (1.0 - beta_one**step_count)
    second_hat = second_new / (1.0 - beta_two**step_count)
    weight_new = weight - learn_rate * (
        first_hat / (jnp.sqrt(second_hat) + epsilon) + decay_rate * weight
    )
    return (weight_new, first_new, second_new)


def device(x, yl, c, z, yh):
    return ((x * 2 + yl) * 2 + c, z * 2 + yh)


def kernel(
    gate_hbm, up_hbm, og_hbm, w_hbm, m_hbm, v_hbm,
    gg_hbm, gu_hbm, grad_out, mv_out, wt_out,
    gate, up, w32, m32, v32, wb, mvb, og_all, h_own, h_all, w_all,
    part, rs, summed, hg, hg_all, gg, gu,
    load_sem, store_sem,
    ogy_s, ogy_r, ogz_s, ogz_r, ogc_s, ogc_r, h_s, h_r, w_s, w_r, wx_s, wx_r, mv_s, mv_r,
    hg_s, hg_r, wt_s, wt_r, rs_s, rs_r, g_s, g_r,
):
    d = lax.axis_index("dp")
    q = lax.axis_index("tensor")
    p = d // 2
    c = lax.rem(d, 2)
    x = p // 2
    yl = lax.rem(p, 2)
    z = q // 2
    yh = lax.rem(q, 2)
    tok, ff = gate.shape
    blk = w32.shape[0]
    cols = w32.shape[1]
    sub = cols // 16
    rows = 4 * blk
    tq = tok // 4
    mine = 2 * yl + c
    diag = p == q
    diag_i = jnp.where(diag, 1, 0)

    def mult(v, n):
        return pl.multiple_of(v, n)

    def peer(r):
        pyl = lax.rem(yl + r % 2, 2)
        pc = lax.rem(c + r // 2, 2)
        return device(x, pyl, pc, z, yh), 2 * pyl + pc

    def across(r):
        return lax.rem(x + r, 4)

    loads = [
        pltpu.make_async_copy(og_hbm, og_all.at[pl.ds(mult(mine * tok, tok), tok)], load_sem.at[0]),
        pltpu.make_async_copy(w_hbm, w32, load_sem.at[1]),
        pltpu.make_async_copy(gate_hbm, gate, load_sem.at[2]),
        pltpu.make_async_copy(up_hbm, up, load_sem.at[3]),
        pltpu.make_async_copy(m_hbm, m32, load_sem.at[4]),
        pltpu.make_async_copy(v_hbm, v32, load_sem.at[5]),
    ]
    for load in loads:
        load.start()

    barrier = pltpu.get_barrier_semaphore()

    @pl.loop(0, 16)
    def _(n):
        @pl.when(jnp.logical_not(jnp.logical_and(diag, n == d)))
        def _():
            pl.semaphore_signal(barrier, inc=1, device_id=(n, p), device_id_type=MESH)

        sd = 2 * q + n // 8
        st = lax.rem(n, 8)

        @pl.when(jnp.logical_not(jnp.logical_and(sd == d, st == q)))
        def _():
            pl.semaphore_signal(barrier, inc=1, device_id=(sd, st), device_id_type=MESH)

    for r in range(1, 4):
        pl.semaphore_signal(barrier, inc=1, device_id=peer(r)[0], device_id_type=MESH)
        pl.semaphore_signal(
            barrier, inc=1, device_id=device(across(r), yl, c, z, yh), device_id_type=MESH
        )
        pl.semaphore_signal(
            barrier, inc=1, device_id=device(x, yl, c, lax.rem(z + r, 4), yh), device_id_type=MESH
        )

    loads[0].wait()
    loads[1].wait()
    for n in range(4):
        wb[n] = w32[:, n * 4 * sub : (n + 1) * 4 * sub].astype(BF16)
    pl.semaphore_wait(barrier, 41 - 2 * diag_i)

    def remote(src, dst, ss, rr, to):
        return pltpu.make_async_remote_copy(
            src_ref=src, dst_ref=dst, send_sem=ss, recv_sem=rr, device_id=to, device_id_type=MESH
        )

    sends = []

    def go(*args):
        copy = remote(*args)
        copy.start()
        sends.append(copy)

    half = tq // 2

    def og_half(slot, part_index, side_half):
        start = mult(slot * tok + part_index * tq + side_half * half, half)
        return og_all.at[pl.ds(start, half)]

    def og_slot(slot):
        return og_all.at[pl.ds(mult(slot * tok, tok), tok)]

    side, side_slot = peer(1)
    core, core_slot = peer(2)
    _, far_slot = peer(3)
    for i in range(2):
        mine_half = og_half(mine, z, i)
        go(mine_half, mine_half, ogy_s.at[i], ogy_r.at[i], side)

    block = 2 * lax.rem(z, 2) + yh
    w_core = z // 2
    self_w = jnp.logical_and(diag, jnp.logical_and(c == yl, w_core == c))

    def w_cols(at_x):
        return pl.ds(mult(at_x * 4 * sub, 128), 4 * sub)

    def w_place(at_x):
        return w_all.at[pl.ds(mult(block * blk, blk), blk), w_cols(at_x)]

    for r in (1, 3, 2):
        go(wb.at[across(r)], w_place(across(r)), w_s.at[r], w_r.at[block],
           device(across(r), c, w_core, x, yl))
    w_home = remote(wb.at[x], w_place(x), w_s.at[0], w_r.at[block], device(x, c, w_core, x, yl))

    @pl.when(self_w)
    def _():
        pltpu.make_async_copy(wb.at[x], w_place(x), w_r.at[block]).start()

    @pl.when(jnp.logical_not(self_w))
    def _():
        w_home.start()

    go(og_slot(mine), og_slot(mine), ogc_s.at[8], ogc_r.at[8], core)

    loads[4].wait()
    loads[5].wait()
    for n in range(16):
        mvb[n, 0] = m32[:, n * sub : (n + 1) * sub].astype(BF16)
        mvb[n, 1] = v32[:, n * sub : (n + 1) * sub].astype(BF16)
    mv_dst = mv_out.at[:, pl.ds(mult((8 * c + q) * blk, blk), blk), :]

    @pl.when(diag)
    def _():
        pltpu.make_async_copy(mvb.at[d], mv_dst, mv_r).start()

    @pl.when(jnp.logical_not(diag))
    def _():
        remote(mvb.at[d], mv_dst, mv_s.at[0], mv_r, (d, p)).start()

    @pl.loop(0, 4)
    def _(k):
        for r in (1, 3, 2, 0):
            n = across(r) * 4 + lax.rem(mine + k, 4)
            i = k * 4 + r

            @pl.when(i > 0)
            def _():
                remote(mvb.at[n], mv_dst, mv_s.at[i], mv_r, (n, p)).start()

    loads[2].wait()
    loads[3].wait()

    @pl.loop(0, ff // 128)
    def _(b):
        at = pl.ds(mult(b * 128, 128), 128)
        g = gate[:, at].astype(F32)
        u = up[:, at].astype(F32)
        h = g * jax.nn.sigmoid(g) * u
        h_own[at, :] = h.T.astype(BF16)

    my_cols = pl.ds(mult(mine * tok, 128), tok)
    for r in range(1, 4):
        to, slot = peer(r)
        go(h_own.at[pl.ds(mult(slot * rows, rows), rows)], h_all.at[:, my_cols],
           h_s.at[r - 1], h_r.at[r - 1], to)
    h_all[:, my_cols] = h_own[pl.ds(mult(mine * rows, rows), rows), :]

    z_next = device(x, yl, c, lax.rem(z + 1, 4), yh)
    z_prev = device(x, yl, c, lax.rem(z + 3, 4), yh)
    x_next = device(across(1), yl, c, z, yh)
    x_prev = device(across(3), yl, c, z, yh)

    def quarter(r):
        return lax.rem(z + 4 - r, 4)

    def z_piece(i):
        return og_half(side_slot, quarter((1, 1, 3, 3, 2, 2)[i]), i % 2)

    def z_wait(i):
        got = z_piece(i)
        remote(got, got, ogz_s.at[i], ogz_r.at[i], z_next).wait_recv()
        if i == 0:
            go(got, got, ogz_s.at[4], ogz_r.at[4], z_next)
        if i == 3:
            go(got, got, ogz_s.at[5], ogz_r.at[5], z_prev)
        go(got, got, ogc_s.at[2 + i], ogc_r.at[2 + i], core)

    def y_wait(i):
        got = og_half(side_slot, z, i)
        remote(got, got, ogy_s.at[i], ogy_r.at[i], side).wait_recv()
        up_z = (got, got, ogz_s.at[i], ogz_r.at[i], z_next)
        down_z = (got, got, ogz_s.at[2 + i], ogz_r.at[2 + i], z_prev)
        for which in ((up_z, down_z), (down_z, up_z))[i]:
            go(*which)
        go(got, got, ogc_s.at[i], ogc_r.at[i], core)

    half_rows = rows // 2

    def w_half(at_x, i):
        return w_all.at[pl.ds(i * half_rows, half_rows), w_cols(at_x)]

    def wx_piece(i):
        return w_half(across((3, 3, 1, 1, 2, 2)[i]), i % 2)

    def wx_wait(i):
        got = wx_piece(i)
        remote(got, got, wx_s.at[i], wx_r.at[i], x_next).wait_recv()
        if i == 0:
            go(got, got, wx_s.at[4], wx_r.at[4], x_next)
        if i == 3:
            go(got, got, wx_s.at[5], wx_r.at[5], x_prev)

    y_wait(0)
    for i in range(4):
        there = w_all.at[pl.ds(i * blk, blk), w_cols(x)]
        remote(there, there, w_s.at[0], w_r.at[i], side).wait_recv()
    for i in range(2):
        got = w_half(x, i)
        mate = w_half(x, 1 - i)
        go(got, got, wx_s.at[i], wx_r.at[i], x_next)
        go(mate, mate, wx_s.at[3 - i], wx_r.at[3 - i], x_prev)
    y_wait(1)
    z_wait(0)
    z_wait(3)
    wx_wait(0)
    wx_wait(3)
    for i in (1, 2, 4, 5):
        z_wait(i)

    for r in range(1, 4):
        _, slot = peer(r)
        there = h_all.at[:, pl.ds(mult(slot * tok, 128), tok)]
        remote(there, there, h_s.at[r - 1], h_r.at[r - 1], side).wait_recv()
    remote(og_slot(core_slot), og_slot(core_slot), ogc_s.at[8], ogc_r.at[8], core).wait_recv()
    for i in range(8):
        got = og_half(far_slot, quarter((0, 0, 1, 1, 3, 3, 2, 2)[i]), i % 2)
        remote(got, got, ogc_s.at[i], ogc_r.at[i], core).wait_recv()

    @pl.loop(0, 4)
    def _(k):
        for r in (1, 3, 2, 0):
            to_x = across(r)
            at = pl.ds(mult((to_x * 4 + k) * sub, 128), sub)
            part[r, k] = jnp.dot(
                h_all[...], og_all[:, at], preferred_element_type=F32
            ).astype(BF16)
            if r:
                remote(part.at[r, k], rs.at[r - 1, k], rs_s.at[r - 1, k], rs_r.at[r - 1, k],
                       device(to_x, yl, c, z, yh)).start()

    for i in (1, 2, 4, 5):
        wx_wait(i)
    my_rows = pl.ds(mult(mine * rows, rows), rows)
    for r in range(1, 4):
        to, k = peer(r)
        go(w_all.at[:, pl.ds(mult((x * 4 + k) * sub, 128), sub)], wt_out.at[my_rows],
           wt_s.at[r - 1], wt_r.at[r - 1], to)
    wt_own = pltpu.make_async_copy(
        w_all.at[:, pl.ds(mult(d * sub, 128), sub)], wt_out.at[my_rows], store_sem.at[0]
    )
    wt_own.start()

    n_tile = 4 * tok // 6

    @pl.loop(0, 6)
    def _(n):
        at = pl.ds(mult(n * n_tile, n_tile), n_tile)
        hg[:, at] = lax.dot_general(
            w_all[...], og_all[at, :], (((1,), (1,)), ((), ())), preferred_element_type=F32
        ).astype(BF16)

    for r in range(1, 4):
        to, slot = peer(r)
        go(hg.at[:, pl.ds(mult(slot * tok, 128), tok)], hg_all.at[my_rows],
           hg_s.at[r - 1], hg_r.at[r - 1], to)
    hg_all[my_rows, :] = hg[:, my_cols]

    def reduce_chunk(k):
        for r in range(3):
            remote(rs.at[r, k], rs.at[r, k], rs_s.at[r, k], rs_r.at[r, k], side).wait_recv()
        summed[k] = (
            part[0, k].astype(F32) + rs[0, k].astype(F32)
            + (rs[1, k].astype(F32) + rs[2, k].astype(F32))
        ).astype(BF16)
        k_yl = k // 2
        k_c = k % 2
        r = (1 - jnp.where(k_yl == yl, 1, 0)) + 2 * (1 - jnp.where(k_c == c, 1, 0))
        local = r == 0
        dst = grad_out.at[my_rows]

        @pl.when(local)
        def _():
            pltpu.make_async_copy(summed.at[k], dst, store_sem.at[1]).start()

        @pl.when(jnp.logical_not(local))
        def _():
            remote(summed.at[k], dst, g_s.at[r], g_r.at[r], device(x, k_yl, k_c, z, yh)).start()

    def finish_grads():
        for r in range(1, 4):
            _, slot = peer(r)
            there = hg_all.at[pl.ds(mult(slot * rows, rows), rows)]
            remote(there, there, hg_s.at[r - 1], hg_r.at[r - 1], side).wait_recv()

        @pl.loop(0, ff // 128)
        def _(b):
            at = pl.ds(mult(b * 128, 128), 128)
            back = hg_all[at, :].astype(F32).T
            g = gate[:, at].astype(F32)
            u = up[:, at].astype(F32)
            s = jax.nn.sigmoid(g)
            gg[:, at] = (back * u * s * (1.0 + g * (1.0 - s))).astype(BF16)
            gu[:, at] = (back * g * s).astype(BF16)

        pltpu.make_async_copy(gg, gg_hbm, store_sem.at[2]).start()
        pltpu.make_async_copy(gu, gu_hbm, store_sem.at[3]).start()

    for k in range(4):
        if k == 3:
            finish_grads()
        reduce_chunk(k)

    for copy in sends:
        copy.wait_send()

    @pl.when(jnp.logical_not(self_w))
    def _():
        w_home.wait_send()

    @pl.when(jnp.logical_not(diag))
    def _():
        remote(mvb.at[0], mv_dst, mv_s.at[0], mv_r, side).wait_send()

    for r in range(1, 16):
        remote(mvb.at[r], mv_dst, mv_s.at[r], mv_r, side).wait_send()
    for r in range(3):
        for k in range(4):
            remote(part.at[r + 1, k], rs.at[r, k], rs_s.at[r, k], rs_r.at[r, k], side).wait_send()
    pltpu.make_async_copy(gg, gg_hbm, store_sem.at[2]).wait()
    pltpu.make_async_copy(gu, gu_hbm, store_sem.at[3]).wait()
    wt_own.wait()
    pltpu.make_async_copy(summed.at[0], grad_out.at[my_rows], store_sem.at[1]).wait()
    for r in range(1, 4):
        _, slot = peer(r)
        there = pl.ds(mult(slot * rows, rows), rows)
        remote(wt_out.at[there], wt_out.at[there], wt_s.at[r - 1], wt_r.at[r - 1], side).wait_recv()
        remote(summed.at[r], grad_out.at[there], g_s.at[r], g_r.at[r], side).wait()
    remote(mv_out, mv_out, mv_s.at[0], mv_r, side).wait_recv()


def body(gate_pre, up_pre, out_grad, old_weight, old_first, old_second):
    tok, ff = gate_pre.shape
    blk, cols = old_weight.shape
    rows = 4 * blk
    sub = cols // 16
    anyspec = pl.BlockSpec(memory_space=pl.ANY)
    dma = pltpu.SemaphoreType.DMA
    gg, gu, grad, moments, weight = pl.pallas_call(
        kernel,
        out_shape=(
            jax.ShapeDtypeStruct((tok, ff), BF16),
            jax.ShapeDtypeStruct((tok, ff), BF16),
            jax.ShapeDtypeStruct((ff, sub), BF16),
            jax.ShapeDtypeStruct((2, ff, sub), BF16),
            jax.ShapeDtypeStruct((ff, sub), BF16),
        ),
        in_specs=[anyspec] * 6,
        out_specs=(anyspec,) * 5,
        scratch_shapes=[
            pltpu.VMEM((tok, ff), BF16),
            pltpu.VMEM((tok, ff), BF16),
            pltpu.VMEM((blk, cols), F32),
            pltpu.VMEM((blk, cols), F32),
            pltpu.VMEM((blk, cols), F32),
            pltpu.VMEM((4, blk, cols // 4), BF16),
            pltpu.VMEM((16, 2, blk, sub), BF16),
            pltpu.VMEM((4 * tok, cols), BF16),
            pltpu.VMEM((ff, tok), BF16),
            pltpu.VMEM((rows, 4 * tok), BF16),
            pltpu.VMEM((rows, cols), BF16),
            pltpu.VMEM((4, 4, rows, sub), BF16),
            pltpu.VMEM((3, 4, rows, sub), BF16),
            pltpu.VMEM((4, rows, sub), BF16),
            pltpu.VMEM((rows, 4 * tok), BF16),
            pltpu.VMEM((ff, tok), BF16),
            pltpu.VMEM((tok, ff), BF16),
            pltpu.VMEM((tok, ff), BF16),
            dma((6,)),
            dma((4,)),
            dma((2,)), dma((2,)),
            dma((6,)), dma((6,)),
            dma((9,)), dma((9,)),
            dma((3,)), dma((3,)),
            dma((4,)), dma((4,)),
            dma((6,)), dma((6,)),
            dma((16,)), dma(()),
            dma((3,)), dma((3,)),
            dma((3,)), dma((3,)),
            dma((3, 4)), dma((3, 4)),
            dma((4,)), dma((4,)),
        ],
        compiler_params=pltpu.CompilerParams(
            collective_id=0, has_side_effects=True, vmem_limit_bytes=60 << 20
        ),
        cost_estimate=pl.CostEstimate(
            flops=4 * tok * ff * cols, bytes_accessed=6 * tok * ff * 2, transcendentals=2 * tok * ff
        ),
        name="step",
    )(gate_pre, up_pre, out_grad, old_weight, old_first, old_second)
    new_weight, new_first, new_second = adamw(
        weight.astype(F32), moments[0].astype(F32), moments[1].astype(F32), grad.astype(F32)
    )
    return (new_weight, new_first, new_second, gg, gu)


def solution(mesh):
    placed = (
        P("dp", "tensor"),
        P("dp", "tensor"),
        P("dp", None),
        P(("dp", "tensor"), None),
        P(("dp", "tensor"), None),
        P(("dp", "tensor"), None),
    )
    return jax.shard_map(
        body,
        mesh=mesh,
        in_specs=placed,
        out_specs=(
            P("tensor", "dp"),
            P("tensor", "dp"),
            P("tensor", "dp"),
            P("dp", "tensor"),
            P("dp", "tensor"),
        ),
        check_vma=False,
    )
```

```python
import functools
import jax
import jax.numpy as jnp
from jax import lax
from jax.experimental import pallas as pl
from jax.experimental.pallas import tpu as pltpu
from jax.sharding import PartitionSpec as P

beta_one = 0.9
beta_two = 0.95
learn_rate = 0.0003
decay_rate = 0.1
epsilon = 1e-08
step_count = 1001

MESH = pl.DeviceIdType.MESH
BF16 = jnp.bfloat16
F32 = jnp.float32


def adamw(weight, first, second, grad):
    first_new = beta_one * first + (1.0 - beta_one) * grad
    second_new = beta_two * second + (1.0 - beta_two) * grad * grad
    first_hat = first_new / (1.0 - beta_one**step_count)
    second_hat = second_new / (1.0 - beta_two**step_count)
    weight_new = weight - learn_rate * (
        first_hat / (jnp.sqrt(second_hat) + epsilon) + decay_rate * weight
    )
    return (weight_new, first_new, second_new)


def device(x, yl, c, z, yh):
    return ((x * 2 + yl) * 2 + c, z * 2 + yh)


def kernel(
    gate_hbm, up_hbm, og_hbm, w_hbm, m_hbm, v_hbm,
    gg_hbm, gu_hbm, grad_out, mv_out, wt_out,
    gate, up, w32, m32, v32, wb, mvb, og_all, h_own, h_all, w_all,
    part, rs, mid, rs2, summed, hg, hg_all, gg, gu,
    load_sem, store_sem,
    ogy_s, ogy_r, ogz_s, ogz_r, ogc_s, ogc_r, h_s, h_r, w_s, w_r, wx_s, wx_r, mv_s, mv_r,
    hg_s, hg_r, wt_s, wt_r, rs_s, rs_r, rs2_s, rs2_r, g_s, g_r,
):
    d = lax.axis_index("dp")
    q = lax.axis_index("tensor")
    p = d // 2
    c = lax.rem(d, 2)
    x = p // 2
    yl = lax.rem(p, 2)
    z = q // 2
    yh = lax.rem(q, 2)
    tok, ff = gate.shape
    blk = w32.shape[0]
    cols = w32.shape[1]
    sub = cols // 16
    rows = 4 * blk
    tq = tok // 4
    mine = 2 * yl + c
    diag = p == q
    diag_i = jnp.where(diag, 1, 0)

    def mult(v, n):
        return pl.multiple_of(v, n)

    def peer(r):
        pyl = lax.rem(yl + r % 2, 2)
        pc = lax.rem(c + r // 2, 2)
        return device(x, pyl, pc, z, yh), 2 * pyl + pc

    def across(r):
        return lax.rem(x + r, 4)

    loads = [
        pltpu.make_async_copy(og_hbm, og_all.at[pl.ds(mult(mine * tok, tok), tok)], load_sem.at[0]),
        pltpu.make_async_copy(w_hbm, w32, load_sem.at[1]),
        pltpu.make_async_copy(gate_hbm, gate, load_sem.at[2]),
        pltpu.make_async_copy(up_hbm, up, load_sem.at[3]),
        pltpu.make_async_copy(m_hbm, m32, load_sem.at[4]),
        pltpu.make_async_copy(v_hbm, v32, load_sem.at[5]),
    ]
    for load in loads:
        load.start()

    barrier = pltpu.get_barrier_semaphore()

    @pl.loop(0, 16)
    def _(n):
        @pl.when(jnp.logical_not(jnp.logical_and(diag, n == d)))
        def _():
            pl.semaphore_signal(barrier, inc=1, device_id=(n, p), device_id_type=MESH)

        sd = 2 * q + n // 8
        st = lax.rem(n, 8)

        @pl.when(jnp.logical_not(jnp.logical_and(sd == d, st == q)))
        def _():
            pl.semaphore_signal(barrier, inc=1, device_id=(sd, st), device_id_type=MESH)

    for r in range(1, 4):
        pl.semaphore_signal(barrier, inc=1, device_id=peer(r)[0], device_id_type=MESH)
        pl.semaphore_signal(
            barrier, inc=1, device_id=device(across(r), yl, c, z, yh), device_id_type=MESH
        )
        pl.semaphore_signal(
            barrier, inc=1, device_id=device(x, yl, c, lax.rem(z + r, 4), yh), device_id_type=MESH
        )

    loads[0].wait()
    loads[1].wait()
    for n in range(4):
        wb[n] = w32[:, n * 4 * sub : (n + 1) * 4 * sub].astype(BF16)
    pl.semaphore_wait(barrier, 41 - 2 * diag_i)

    def remote(src, dst, ss, rr, to):
        return pltpu.make_async_remote_copy(
            src_ref=src, dst_ref=dst, send_sem=ss, recv_sem=rr, device_id=to, device_id_type=MESH
        )

    sends = []

    def go(*args):
        copy = remote(*args)
        copy.start()
        sends.append(copy)

    half = tq // 2

    def og_half(slot, part_index, side_half):
        start = mult(slot * tok + part_index * tq + side_half * half, half)
        return og_all.at[pl.ds(start, half)]

    def og_slot(slot):
        return og_all.at[pl.ds(mult(slot * tok, tok), tok)]

    side, side_slot = peer(1)
    core, core_slot = peer(2)
    _, far_slot = peer(3)
    for i in range(2):
        mine_half = og_half(mine, z, i)
        go(mine_half, mine_half, ogy_s.at[i], ogy_r.at[i], side)

    block = 2 * lax.rem(z, 2) + yh
    w_core = z // 2
    self_w = jnp.logical_and(diag, jnp.logical_and(c == yl, w_core == c))

    def w_cols(at_x):
        return pl.ds(mult(at_x * 4 * sub, 128), 4 * sub)

    def w_place(at_x):
        return w_all.at[pl.ds(mult(block * blk, blk), blk), w_cols(at_x)]

    for r in (1, 3, 2):
        go(wb.at[across(r)], w_place(across(r)), w_s.at[r], w_r.at[block],
           device(across(r), c, w_core, x, yl))
    w_home = remote(wb.at[x], w_place(x), w_s.at[0], w_r.at[block], device(x, c, w_core, x, yl))

    @pl.when(self_w)
    def _():
        pltpu.make_async_copy(wb.at[x], w_place(x), w_r.at[block]).start()

    @pl.when(jnp.logical_not(self_w))
    def _():
        w_home.start()

    go(og_slot(mine), og_slot(mine), ogc_s.at[8], ogc_r.at[8], core)

    loads[4].wait()
    loads[5].wait()
    for n in range(16):
        mvb[n, 0] = m32[:, n * sub : (n + 1) * sub].astype(BF16)
        mvb[n, 1] = v32[:, n * sub : (n + 1) * sub].astype(BF16)
    mv_dst = mv_out.at[:, pl.ds(mult((8 * c + q) * blk, blk), blk), :]

    @pl.when(diag)
    def _():
        pltpu.make_async_copy(mvb.at[d], mv_dst, mv_r).start()

    @pl.when(jnp.logical_not(diag))
    def _():
        remote(mvb.at[d], mv_dst, mv_s.at[0], mv_r, (d, p)).start()

    @pl.loop(0, 4)
    def _(k):
        for r in (1, 3, 2, 0):
            n = across(r) * 4 + lax.rem(mine + k, 4)
            i = k * 4 + r

            @pl.when(i > 0)
            def _():
                remote(mvb.at[n], mv_dst, mv_s.at[i], mv_r, (n, p)).start()

    loads[2].wait()
    loads[3].wait()

    @pl.loop(0, ff // 128)
    def _(b):
        at = pl.ds(mult(b * 128, 128), 128)
        g = gate[:, at].astype(F32)
        u = up[:, at].astype(F32)
        h = g * jax.nn.sigmoid(g) * u
        h_own[at, :] = h.T.astype(BF16)

    my_cols = pl.ds(mult(mine * tok, 128), tok)
    for r in range(1, 4):
        to, slot = peer(r)
        go(h_own.at[pl.ds(mult(slot * rows, rows), rows)], h_all.at[:, my_cols],
           h_s.at[r - 1], h_r.at[r - 1], to)
    h_all[:, my_cols] = h_own[pl.ds(mult(mine * rows, rows), rows), :]

    z_next = device(x, yl, c, lax.rem(z + 1, 4), yh)
    z_prev = device(x, yl, c, lax.rem(z + 3, 4), yh)
    x_next = device(across(1), yl, c, z, yh)
    x_prev = device(across(3), yl, c, z, yh)

    def quarter(r):
        return lax.rem(z + 4 - r, 4)

    def z_piece(i):
        return og_half(side_slot, quarter((1, 1, 3, 3, 2, 2)[i]), i % 2)

    def z_wait(i):
        got = z_piece(i)
        remote(got, got, ogz_s.at[i], ogz_r.at[i], z_next).wait_recv()
        if i == 0:
            go(got, got, ogz_s.at[4], ogz_r.at[4], z_next)
        if i == 3:
            go(got, got, ogz_s.at[5], ogz_r.at[5], z_prev)
        go(got, got, ogc_s.at[2 + i], ogc_r.at[2 + i], core)

    def y_wait(i):
        got = og_half(side_slot, z, i)
        remote(got, got, ogy_s.at[i], ogy_r.at[i], side).wait_recv()
        up_z = (got, got, ogz_s.at[i], ogz_r.at[i], z_next)
        down_z = (got, got, ogz_s.at[2 + i], ogz_r.at[2 + i], z_prev)
        for which in ((up_z, down_z), (down_z, up_z))[i]:
            go(*which)
        go(got, got, ogc_s.at[i], ogc_r.at[i], core)

    half_rows = rows // 2

    def w_half(at_x, i):
        return w_all.at[pl.ds(i * half_rows, half_rows), w_cols(at_x)]

    def wx_piece(i):
        return w_half(across((3, 3, 1, 1, 2, 2)[i]), i % 2)

    def wx_wait(i):
        got = wx_piece(i)
        remote(got, got, wx_s.at[i], wx_r.at[i], x_next).wait_recv()
        if i == 0:
            go(got, got, wx_s.at[4], wx_r.at[4], x_next)
        if i == 3:
            go(got, got, wx_s.at[5], wx_r.at[5], x_prev)

    y_wait(0)
    for i in range(4):
        there = w_all.at[pl.ds(i * blk, blk), w_cols(x)]
        remote(there, there, w_s.at[0], w_r.at[i], side).wait_recv()
    for i in range(2):
        got = w_half(x, i)
        mate = w_half(x, 1 - i)
        go(got, got, wx_s.at[i], wx_r.at[i], x_next)
        go(mate, mate, wx_s.at[3 - i], wx_r.at[3 - i], x_prev)
    y_wait(1)
    z_wait(0)
    z_wait(3)
    wx_wait(0)
    wx_wait(3)
    for i in (1, 2, 4, 5):
        z_wait(i)

    for r in range(1, 4):
        _, slot = peer(r)
        there = h_all.at[:, pl.ds(mult(slot * tok, 128), tok)]
        remote(there, there, h_s.at[r - 1], h_r.at[r - 1], side).wait_recv()
    remote(og_slot(core_slot), og_slot(core_slot), ogc_s.at[8], ogc_r.at[8], core).wait_recv()
    for i in range(8):
        got = og_half(far_slot, quarter((0, 0, 1, 1, 3, 3, 2, 2)[i]), i % 2)
        remote(got, got, ogc_s.at[i], ogc_r.at[i], core).wait_recv()

    near = x + 1 - 2 * lax.rem(x, 2)
    far = 3 - x
    opposite = 3 - near

    def at_x(other):
        return device(other, yl, c, z, yh)

    @pl.loop(0, 4)
    def _(k):
        odd = lax.rem(k, 2)
        first = jnp.where(odd == 1, far, near)
        second = jnp.where(odd == 1, near, far)
        for i, to_x in enumerate((first, opposite, x, second)):
            at = pl.ds(mult((to_x * 4 + k) * sub, 128), sub)
            part[k, i] = jnp.dot(h_all[...], og_all[:, at], preferred_element_type=F32).astype(BF16)
            if i == 1:
                remote(part.at[k, pl.ds(0, 2)], rs.at[k], rs_s.at[k], rs_r.at[k], at_x(first)).start()

    def middle(k):
        remote(rs.at[k], rs.at[k], rs_s.at[k], rs_r.at[k], side).wait_recv()
        mid[k] = (part[k, 3].astype(F32) + rs[k, 1].astype(F32)).astype(BF16)
        go(mid.at[k], rs2.at[k], rs2_s.at[k], rs2_r.at[k], at_x((far, near)[k % 2]))

    for i in (1, 2, 4, 5):
        wx_wait(i)
    my_rows = pl.ds(mult(mine * rows, rows), rows)
    for r in range(1, 4):
        to, k = peer(r)
        go(w_all.at[:, pl.ds(mult((x * 4 + k) * sub, 128), sub)], wt_out.at[my_rows],
           wt_s.at[r - 1], wt_r.at[r - 1], to)
    wt_own = pltpu.make_async_copy(
        w_all.at[:, pl.ds(mult(d * sub, 128), sub)], wt_out.at[my_rows], store_sem.at[0]
    )
    wt_own.start()

    n_tile = 4 * tok // 6

    @pl.loop(0, 6)
    def _(n):
        at = pl.ds(mult(n * n_tile, n_tile), n_tile)
        hg[:, at] = lax.dot_general(
            w_all[...], og_all[at, :], (((1,), (1,)), ((), ())), preferred_element_type=F32
        ).astype(BF16)

    for r in range(1, 4):
        to, slot = peer(r)
        go(hg.at[:, pl.ds(mult(slot * tok, 128), tok)], hg_all.at[my_rows],
           hg_s.at[r - 1], hg_r.at[r - 1], to)
    hg_all[my_rows, :] = hg[:, my_cols]

    for k in range(4):
        middle(k)

    def reduce_chunk(k):
        remote(rs2.at[k], rs2.at[k], rs2_s.at[k], rs2_r.at[k], side).wait_recv()
        summed[k] = (
            part[k, 2].astype(F32) + rs[k, 0].astype(F32) + rs2[k].astype(F32)
        ).astype(BF16)
        k_yl = k // 2
        k_c = k % 2
        r = (1 - jnp.where(k_yl == yl, 1, 0)) + 2 * (1 - jnp.where(k_c == c, 1, 0))
        local = r == 0
        dst = grad_out.at[my_rows]

        @pl.when(local)
        def _():
            pltpu.make_async_copy(summed.at[k], dst, store_sem.at[1]).start()

        @pl.when(jnp.logical_not(local))
        def _():
            remote(summed.at[k], dst, g_s.at[r], g_r.at[r], device(x, k_yl, k_c, z, yh)).start()

    def finish_grads():
        for r in range(1, 4):
            _, slot = peer(r)
            there = hg_all.at[pl.ds(mult(slot * rows, rows), rows)]
            remote(there, there, hg_s.at[r - 1], hg_r.at[r - 1], side).wait_recv()

        @pl.loop(0, ff // 128)
        def _(b):
            at = pl.ds(mult(b * 128, 128), 128)
            back = hg_all[at, :].astype(F32).T
            g = gate[:, at].astype(F32)
            u = up[:, at].astype(F32)
            s = jax.nn.sigmoid(g)
            gg[:, at] = (back * u * s * (1.0 + g * (1.0 - s))).astype(BF16)
            gu[:, at] = (back * g * s).astype(BF16)

        pltpu.make_async_copy(gg, gg_hbm, store_sem.at[2]).start()
        pltpu.make_async_copy(gu, gu_hbm, store_sem.at[3]).start()

    for k in range(4):
        if k == 3:
            finish_grads()
        reduce_chunk(k)

    for copy in sends:
        copy.wait_send()

    @pl.when(jnp.logical_not(self_w))
    def _():
        w_home.wait_send()

    @pl.when(jnp.logical_not(diag))
    def _():
        remote(mvb.at[0], mv_dst, mv_s.at[0], mv_r, side).wait_send()

    for r in range(1, 16):
        remote(mvb.at[r], mv_dst, mv_s.at[r], mv_r, side).wait_send()
    for k in range(4):
        remote(part.at[k, pl.ds(0, 2)], rs.at[k], rs_s.at[k], rs_r.at[k], side).wait_send()
    pltpu.make_async_copy(gg, gg_hbm, store_sem.at[2]).wait()
    pltpu.make_async_copy(gu, gu_hbm, store_sem.at[3]).wait()
    wt_own.wait()
    pltpu.make_async_copy(summed.at[0], grad_out.at[my_rows], store_sem.at[1]).wait()
    for r in range(1, 4):
        _, slot = peer(r)
        there = pl.ds(mult(slot * rows, rows), rows)
        remote(wt_out.at[there], wt_out.at[there], wt_s.at[r - 1], wt_r.at[r - 1], side).wait_recv()
        remote(summed.at[r], grad_out.at[there], g_s.at[r], g_r.at[r], side).wait()
    remote(mv_out, mv_out, mv_s.at[0], mv_r, side).wait_recv()


def body(gate_pre, up_pre, out_grad, old_weight, old_first, old_second):
    tok, ff = gate_pre.shape
    blk, cols = old_weight.shape
    rows = 4 * blk
    sub = cols // 16
    anyspec = pl.BlockSpec(memory_space=pl.ANY)
    dma = pltpu.SemaphoreType.DMA
    gg, gu, grad, moments, weight = pl.pallas_call(
        kernel,
        out_shape=(
            jax.ShapeDtypeStruct((tok, ff), BF16),
            jax.ShapeDtypeStruct((tok, ff), BF16),
            jax.ShapeDtypeStruct((ff, sub), BF16),
            jax.ShapeDtypeStruct((2, ff, sub), BF16),
            jax.ShapeDtypeStruct((ff, sub), BF16),
        ),
        in_specs=[anyspec] * 6,
        out_specs=(anyspec,) * 5,
        scratch_shapes=[
            pltpu.VMEM((tok, ff), BF16),
            pltpu.VMEM((tok, ff), BF16),
            pltpu.VMEM((blk, cols), F32),
            pltpu.VMEM((blk, cols), F32),
            pltpu.VMEM((blk, cols), F32),
            pltpu.VMEM((4, blk, cols // 4), BF16),
            pltpu.VMEM((16, 2, blk, sub), BF16),
            pltpu.VMEM((4 * tok, cols), BF16),
            pltpu.VMEM((ff, tok), BF16),
            pltpu.VMEM((rows, 4 * tok), BF16),
            pltpu.VMEM((rows, cols), BF16),
            pltpu.VMEM((4, 4, rows, sub), BF16),
            pltpu.VMEM((4, 2, rows, sub), BF16),
            pltpu.VMEM((4, rows, sub), BF16),
            pltpu.VMEM((4, rows, sub), BF16),
            pltpu.VMEM((4, rows, sub), BF16),
            pltpu.VMEM((rows, 4 * tok), BF16),
            pltpu.VMEM((ff, tok), BF16),
            pltpu.VMEM((tok, ff), BF16),
            pltpu.VMEM((tok, ff), BF16),
            dma((6,)),
            dma((4,)),
            dma((2,)), dma((2,)),
            dma((6,)), dma((6,)),
            dma((9,)), dma((9,)),
            dma((3,)), dma((3,)),
            dma((4,)), dma((4,)),
            dma((6,)), dma((6,)),
            dma((16,)), dma(()),
            dma((3,)), dma((3,)),
            dma((3,)), dma((3,)),
            dma((4,)), dma((4,)),
            dma((4,)), dma((4,)),
            dma((4,)), dma((4,)),
        ],
        compiler_params=pltpu.CompilerParams(
            collective_id=0, has_side_effects=True, vmem_limit_bytes=60 << 20
        ),
        cost_estimate=pl.CostEstimate(
            flops=4 * tok * ff * cols, bytes_accessed=6 * tok * ff * 2, transcendentals=2 * tok * ff
        ),
        name="step",
    )(gate_pre, up_pre, out_grad, old_weight, old_first, old_second)
    new_weight, new_first, new_second = adamw(
        weight.astype(F32), moments[0].astype(F32), moments[1].astype(F32), grad.astype(F32)
    )
    return (new_weight, new_first, new_second, gg, gu)


def solution(mesh):
    placed = (
        P("dp", "tensor"),
        P("dp", "tensor"),
        P("dp", None),
        P(("dp", "tensor"), None),
        P(("dp", "tensor"), None),
        P(("dp", "tensor"), None),
    )
    return jax.shard_map(
        body,
        mesh=mesh,
        in_specs=placed,
        out_specs=(
            P("tensor", "dp"),
            P("tensor", "dp"),
            P("tensor", "dp"),
            P("dp", "tensor"),
            P("dp", "tensor"),
        ),
        check_vma=False,
    )
```

```python
import functools
import jax
import jax.numpy as jnp
from jax import lax
from jax.experimental import pallas as pl
from jax.experimental.pallas import tpu as pltpu
from jax.sharding import PartitionSpec as P

beta_one = 0.9
beta_two = 0.95
learn_rate = 0.0003
decay_rate = 0.1
epsilon = 1e-08
step_count = 1001

MESH = pl.DeviceIdType.MESH
BF16 = jnp.bfloat16
F32 = jnp.float32


def adamw(weight, first, second, grad):
    first_new = beta_one * first + (1.0 - beta_one) * grad
    second_new = beta_two * second + (1.0 - beta_two) * grad * grad
    first_hat = first_new / (1.0 - beta_one**step_count)
    second_hat = second_new / (1.0 - beta_two**step_count)
    weight_new = weight - learn_rate * (
        first_hat / (jnp.sqrt(second_hat) + epsilon) + decay_rate * weight
    )
    return (weight_new, first_new, second_new)


def device(x, yl, c, z, yh):
    return ((x * 2 + yl) * 2 + c, z * 2 + yh)


def kernel(
    gate_hbm, up_hbm, og_hbm, w_hbm, m_hbm, v_hbm,
    gg_hbm, gu_hbm, grad_out, mv_out, wt_out,
    gate, up, w32, m32, v32, wb, mvb, og_all, h_own, h_all, w_all,
    part, rs, mid, rs2, summed, hg, hg_all, gg, gu,
    load_sem, store_sem,
    ogy_s, ogy_r, ogz_s, ogz_r, ogc_s, ogc_r, h_s, h_r, w_s, w_r, wx_s, wx_r, mv_s, mv_r,
    hg_s, hg_r, wt_s, wt_r, rs_s, rs_r, rs2_s, rs2_r, g_s, g_r,
):
    d = lax.axis_index("dp")
    q = lax.axis_index("tensor")
    p = d // 2
    c = lax.rem(d, 2)
    x = p // 2
    yl = lax.rem(p, 2)
    z = q // 2
    yh = lax.rem(q, 2)
    tok, ff = gate.shape
    blk = w32.shape[0]
    cols = w32.shape[1]
    sub = cols // 16
    rows = 4 * blk
    tq = tok // 4
    mine = 2 * yl + c
    diag = p == q
    diag_i = jnp.where(diag, 1, 0)

    def mult(v, n):
        return pl.multiple_of(v, n)

    def peer(r):
        pyl = lax.rem(yl + r % 2, 2)
        pc = lax.rem(c + r // 2, 2)
        return device(x, pyl, pc, z, yh), 2 * pyl + pc

    def across(r):
        return lax.rem(x + r, 4)

    loads = [
        pltpu.make_async_copy(og_hbm, og_all.at[pl.ds(mult(mine * tok, tok), tok)], load_sem.at[0]),
        pltpu.make_async_copy(w_hbm, w32, load_sem.at[1]),
        pltpu.make_async_copy(gate_hbm, gate, load_sem.at[2]),
        pltpu.make_async_copy(up_hbm, up, load_sem.at[3]),
        pltpu.make_async_copy(m_hbm, m32, load_sem.at[4]),
        pltpu.make_async_copy(v_hbm, v32, load_sem.at[5]),
    ]
    for load in loads:
        load.start()

    barrier = pltpu.get_barrier_semaphore()

    @pl.loop(0, 16)
    def _(n):
        @pl.when(jnp.logical_not(jnp.logical_and(diag, n == d)))
        def _():
            pl.semaphore_signal(barrier, inc=1, device_id=(n, p), device_id_type=MESH)

        sd = 2 * q + n // 8
        st = lax.rem(n, 8)

        @pl.when(jnp.logical_not(jnp.logical_and(sd == d, st == q)))
        def _():
            pl.semaphore_signal(barrier, inc=1, device_id=(sd, st), device_id_type=MESH)

    for r in range(1, 4):
        pl.semaphore_signal(barrier, inc=1, device_id=peer(r)[0], device_id_type=MESH)
        pl.semaphore_signal(
            barrier, inc=1, device_id=device(across(r), yl, c, z, yh), device_id_type=MESH
        )
        pl.semaphore_signal(
            barrier, inc=1, device_id=device(x, yl, c, lax.rem(z + r, 4), yh), device_id_type=MESH
        )

    loads[0].wait()
    loads[1].wait()
    for n in range(4):
        wb[n] = w32[:, n * 4 * sub : (n + 1) * 4 * sub].astype(BF16)
    pl.semaphore_wait(barrier, 41 - 2 * diag_i)

    def remote(src, dst, ss, rr, to):
        return pltpu.make_async_remote_copy(
            src_ref=src, dst_ref=dst, send_sem=ss, recv_sem=rr, device_id=to, device_id_type=MESH
        )

    sends = []

    def go(*args):
        copy = remote(*args)
        copy.start()
        sends.append(copy)

    half = tq // 2

    def og_half(slot, part_index, side_half):
        start = mult(slot * tok + part_index * tq + side_half * half, half)
        return og_all.at[pl.ds(start, half)]

    def og_slot(slot):
        return og_all.at[pl.ds(mult(slot * tok, tok), tok)]

    side, side_slot = peer(1)
    core, core_slot = peer(2)
    _, far_slot = peer(3)
    for i in range(2):
        mine_half = og_half(mine, z, i)
        go(mine_half, mine_half, ogy_s.at[i], ogy_r.at[i], side)

    block = 2 * lax.rem(z, 2) + yh
    w_core = z // 2
    self_w = jnp.logical_and(diag, jnp.logical_and(c == yl, w_core == c))

    def w_cols(at_x):
        return pl.ds(mult(at_x * 4 * sub, 128), 4 * sub)

    def w_place(at_x):
        return w_all.at[pl.ds(mult(block * blk, blk), blk), w_cols(at_x)]

    for r in (1, 3, 2):
        go(wb.at[across(r)], w_place(across(r)), w_s.at[r], w_r.at[block],
           device(across(r), c, w_core, x, yl))
    w_home = remote(wb.at[x], w_place(x), w_s.at[0], w_r.at[block], device(x, c, w_core, x, yl))

    @pl.when(self_w)
    def _():
        pltpu.make_async_copy(wb.at[x], w_place(x), w_r.at[block]).start()

    @pl.when(jnp.logical_not(self_w))
    def _():
        w_home.start()

    go(og_slot(mine), og_slot(mine), ogc_s.at[8], ogc_r.at[8], core)

    loads[4].wait()
    loads[5].wait()
    for n in range(16):
        mvb[n, 0] = m32[:, n * sub : (n + 1) * sub].astype(BF16)
        mvb[n, 1] = v32[:, n * sub : (n + 1) * sub].astype(BF16)
    mv_dst = mv_out.at[:, pl.ds(mult((8 * c + q) * blk, blk), blk), :]

    @pl.when(diag)
    def _():
        pltpu.make_async_copy(mvb.at[d], mv_dst, mv_r).start()

    @pl.when(jnp.logical_not(diag))
    def _():
        remote(mvb.at[d], mv_dst, mv_s.at[0], mv_r, (d, p)).start()

    @pl.loop(0, 4)
    def _(k):
        for r in (1, 3, 2, 0):
            n = across(r) * 4 + lax.rem(mine + k, 4)
            i = k * 4 + r

            @pl.when(i > 0)
            def _():
                remote(mvb.at[n], mv_dst, mv_s.at[i], mv_r, (n, p)).start()

    loads[2].wait()
    loads[3].wait()

    @pl.loop(0, ff // 128)
    def _(b):
        at = pl.ds(mult(b * 128, 128), 128)
        g = gate[:, at].astype(F32)
        u = up[:, at].astype(F32)
        h = g * jax.nn.sigmoid(g) * u
        h_own[at, :] = h.T.astype(BF16)

    my_cols = pl.ds(mult(mine * tok, 128), tok)
    for r in range(1, 4):
        to, slot = peer(r)
        go(h_own.at[pl.ds(mult(slot * rows, rows), rows)], h_all.at[:, my_cols],
           h_s.at[r - 1], h_r.at[r - 1], to)
    h_all[:, my_cols] = h_own[pl.ds(mult(mine * rows, rows), rows), :]

    z_next = device(x, yl, c, lax.rem(z + 1, 4), yh)
    z_prev = device(x, yl, c, lax.rem(z + 3, 4), yh)
    x_next = device(across(1), yl, c, z, yh)
    x_prev = device(across(3), yl, c, z, yh)

    def quarter(r):
        return lax.rem(z + 4 - r, 4)

    def z_piece(i):
        return og_half(side_slot, quarter((1, 1, 3, 3, 2, 2)[i]), i % 2)

    def z_wait(i):
        got = z_piece(i)
        remote(got, got, ogz_s.at[i], ogz_r.at[i], z_next).wait_recv()
        if i == 0:
            go(got, got, ogz_s.at[4], ogz_r.at[4], z_next)
        if i == 3:
            go(got, got, ogz_s.at[5], ogz_r.at[5], z_prev)
        go(got, got, ogc_s.at[2 + i], ogc_r.at[2 + i], core)

    def y_wait(i):
        got = og_half(side_slot, z, i)
        remote(got, got, ogy_s.at[i], ogy_r.at[i], side).wait_recv()
        up_z = (got, got, ogz_s.at[i], ogz_r.at[i], z_next)
        down_z = (got, got, ogz_s.at[2 + i], ogz_r.at[2 + i], z_prev)
        for which in ((up_z, down_z), (down_z, up_z))[i]:
            go(*which)
        go(got, got, ogc_s.at[i], ogc_r.at[i], core)

    half_rows = rows // 2

    def w_half(at_x, i):
        return w_all.at[pl.ds(i * half_rows, half_rows), w_cols(at_x)]

    def wx_piece(i):
        return w_half(across((3, 3, 1, 1, 2, 2)[i]), i % 2)

    def wx_wait(i):
        got = wx_piece(i)
        remote(got, got, wx_s.at[i], wx_r.at[i], x_next).wait_recv()
        if i == 0:
            go(got, got, wx_s.at[4], wx_r.at[4], x_next)
        if i == 3:
            go(got, got, wx_s.at[5], wx_r.at[5], x_prev)

    y_wait(0)
    for i in range(4):
        there = w_all.at[pl.ds(i * blk, blk), w_cols(x)]
        remote(there, there, w_s.at[0], w_r.at[i], side).wait_recv()
    for i in range(2):
        got = w_half(x, i)
        mate = w_half(x, 1 - i)
        go(got, got, wx_s.at[i], wx_r.at[i], x_next)
        go(mate, mate, wx_s.at[3 - i], wx_r.at[3 - i], x_prev)
    y_wait(1)
    z_wait(0)
    z_wait(3)
    for i in (1, 2):
        z_wait(i)
    wx_wait(0)
    wx_wait(3)
    for i in (4, 5):
        z_wait(i)

    for r in range(1, 4):
        _, slot = peer(r)
        there = h_all.at[:, pl.ds(mult(slot * tok, 128), tok)]
        remote(there, there, h_s.at[r - 1], h_r.at[r - 1], side).wait_recv()
    remote(og_slot(core_slot), og_slot(core_slot), ogc_s.at[8], ogc_r.at[8], core).wait_recv()
    for i in range(8):
        got = og_half(far_slot, quarter((0, 0, 1, 1, 3, 3, 2, 2)[i]), i % 2)
        remote(got, got, ogc_s.at[i], ogc_r.at[i], core).wait_recv()

    near = x + 1 - 2 * lax.rem(x, 2)
    far = 3 - x
    opposite = 3 - near

    def at_x(other):
        return device(other, yl, c, z, yh)

    @pl.loop(0, 4)
    def _(k):
        odd = lax.rem(k, 2)
        first = jnp.where(odd == 1, far, near)
        second = jnp.where(odd == 1, near, far)
        for i, to_x in enumerate((first, opposite, x, second)):
            at = pl.ds(mult((to_x * 4 + k) * sub, 128), sub)
            part[k, i] = jnp.dot(h_all[...], og_all[:, at], preferred_element_type=F32).astype(BF16)
            if i == 1:
                remote(part.at[k, pl.ds(0, 2)], rs.at[k], rs_s.at[k], rs_r.at[k], at_x(first)).start()

    def middle(k):
        remote(rs.at[k], rs.at[k], rs_s.at[k], rs_r.at[k], side).wait_recv()
        mid[k] = (part[k, 3].astype(F32) + rs[k, 1].astype(F32)).astype(BF16)
        go(mid.at[k], rs2.at[k], rs2_s.at[k], rs2_r.at[k], at_x((far, near)[k % 2]))

    for i in (1, 2, 4, 5):
        wx_wait(i)
    my_rows = pl.ds(mult(mine * rows, rows), rows)
    for r in range(1, 4):
        to, k = peer(r)
        go(w_all.at[:, pl.ds(mult((x * 4 + k) * sub, 128), sub)], wt_out.at[my_rows],
           wt_s.at[r - 1], wt_r.at[r - 1], to)
    wt_own = pltpu.make_async_copy(
        w_all.at[:, pl.ds(mult(d * sub, 128), sub)], wt_out.at[my_rows], store_sem.at[0]
    )
    wt_own.start()

    n_tile = 4 * tok // 6

    @pl.loop(0, 6)
    def _(n):
        at = pl.ds(mult(n * n_tile, n_tile), n_tile)
        hg[:, at] = lax.dot_general(
            w_all[...], og_all[at, :], (((1,), (1,)), ((), ())), preferred_element_type=F32
        ).astype(BF16)

    for r in range(1, 4):
        to, slot = peer(r)
        go(hg.at[:, pl.ds(mult(slot * tok, 128), tok)], hg_all.at[my_rows],
           hg_s.at[r - 1], hg_r.at[r - 1], to)
    hg_all[my_rows, :] = hg[:, my_cols]

    for k in range(4):
        middle(k)

    def reduce_chunk(k):
        remote(rs2.at[k], rs2.at[k], rs2_s.at[k], rs2_r.at[k], side).wait_recv()
        summed[k] = (
            part[k, 2].astype(F32) + rs[k, 0].astype(F32) + rs2[k].astype(F32)
        ).astype(BF16)
        k_yl = k // 2
        k_c = k % 2
        r = (1 - jnp.where(k_yl == yl, 1, 0)) + 2 * (1 - jnp.where(k_c == c, 1, 0))
        local = r == 0
        dst = grad_out.at[my_rows]

        @pl.when(local)
        def _():
            pltpu.make_async_copy(summed.at[k], dst, store_sem.at[1]).start()

        @pl.when(jnp.logical_not(local))
        def _():
            remote(summed.at[k], dst, g_s.at[r], g_r.at[r], device(x, k_yl, k_c, z, yh)).start()

    def finish_grads():
        for r in range(1, 4):
            _, slot = peer(r)
            there = hg_all.at[pl.ds(mult(slot * rows, rows), rows)]
            remote(there, there, hg_s.at[r - 1], hg_r.at[r - 1], side).wait_recv()

        @pl.loop(0, ff // 128)
        def _(b):
            at = pl.ds(mult(b * 128, 128), 128)
            back = hg_all[at, :].astype(F32).T
            g = gate[:, at].astype(F32)
            u = up[:, at].astype(F32)
            s = jax.nn.sigmoid(g)
            gg[:, at] = (back * u * s * (1.0 + g * (1.0 - s))).astype(BF16)
            gu[:, at] = (back * g * s).astype(BF16)

        pltpu.make_async_copy(gg, gg_hbm, store_sem.at[2]).start()
        pltpu.make_async_copy(gu, gu_hbm, store_sem.at[3]).start()

    for k in range(4):
        reduce_chunk(k)
    finish_grads()

    for copy in sends:
        copy.wait_send()

    @pl.when(jnp.logical_not(self_w))
    def _():
        w_home.wait_send()

    @pl.when(jnp.logical_not(diag))
    def _():
        remote(mvb.at[0], mv_dst, mv_s.at[0], mv_r, side).wait_send()

    for r in range(1, 16):
        remote(mvb.at[r], mv_dst, mv_s.at[r], mv_r, side).wait_send()
    for k in range(4):
        remote(part.at[k, pl.ds(0, 2)], rs.at[k], rs_s.at[k], rs_r.at[k], side).wait_send()
    pltpu.make_async_copy(gg, gg_hbm, store_sem.at[2]).wait()
    pltpu.make_async_copy(gu, gu_hbm, store_sem.at[3]).wait()
    wt_own.wait()
    pltpu.make_async_copy(summed.at[0], grad_out.at[my_rows], store_sem.at[1]).wait()
    for r in range(1, 4):
        _, slot = peer(r)
        there = pl.ds(mult(slot * rows, rows), rows)
        remote(wt_out.at[there], wt_out.at[there], wt_s.at[r - 1], wt_r.at[r - 1], side).wait_recv()
        remote(summed.at[r], grad_out.at[there], g_s.at[r], g_r.at[r], side).wait()
    remote(mv_out, mv_out, mv_s.at[0], mv_r, side).wait_recv()


def body(gate_pre, up_pre, out_grad, old_weight, old_first, old_second):
    tok, ff = gate_pre.shape
    blk, cols = old_weight.shape
    rows = 4 * blk
    sub = cols // 16
    anyspec = pl.BlockSpec(memory_space=pl.ANY)
    dma = pltpu.SemaphoreType.DMA
    gg, gu, grad, moments, weight = pl.pallas_call(
        kernel,
        out_shape=(
            jax.ShapeDtypeStruct((tok, ff), BF16),
            jax.ShapeDtypeStruct((tok, ff), BF16),
            jax.ShapeDtypeStruct((ff, sub), BF16),
            jax.ShapeDtypeStruct((2, ff, sub), BF16),
            jax.ShapeDtypeStruct((ff, sub), BF16),
        ),
        in_specs=[anyspec] * 6,
        out_specs=(anyspec,) * 5,
        scratch_shapes=[
            pltpu.VMEM((tok, ff), BF16),
            pltpu.VMEM((tok, ff), BF16),
            pltpu.VMEM((blk, cols), F32),
            pltpu.VMEM((blk, cols), F32),
            pltpu.VMEM((blk, cols), F32),
            pltpu.VMEM((4, blk, cols // 4), BF16),
            pltpu.VMEM((16, 2, blk, sub), BF16),
            pltpu.VMEM((4 * tok, cols), BF16),
            pltpu.VMEM((ff, tok), BF16),
            pltpu.VMEM((rows, 4 * tok), BF16),
            pltpu.VMEM((rows, cols), BF16),
            pltpu.VMEM((4, 4, rows, sub), BF16),
            pltpu.VMEM((4, 2, rows, sub), BF16),
            pltpu.VMEM((4, rows, sub), BF16),
            pltpu.VMEM((4, rows, sub), BF16),
            pltpu.VMEM((4, rows, sub), BF16),
            pltpu.VMEM((rows, 4 * tok), BF16),
            pltpu.VMEM((ff, tok), BF16),
            pltpu.VMEM((tok, ff), BF16),
            pltpu.VMEM((tok, ff), BF16),
            dma((6,)),
            dma((4,)),
            dma((2,)), dma((2,)),
            dma((6,)), dma((6,)),
            dma((9,)), dma((9,)),
            dma((3,)), dma((3,)),
            dma((4,)), dma((4,)),
            dma((6,)), dma((6,)),
            dma((16,)), dma(()),
            dma((3,)), dma((3,)),
            dma((3,)), dma((3,)),
            dma((4,)), dma((4,)),
            dma((4,)), dma((4,)),
            dma((4,)), dma((4,)),
        ],
        compiler_params=pltpu.CompilerParams(
            collective_id=0, has_side_effects=True, vmem_limit_bytes=60 << 20
        ),
        cost_estimate=pl.CostEstimate(
            flops=4 * tok * ff * cols, bytes_accessed=6 * tok * ff * 2, transcendentals=2 * tok * ff
        ),
        name="step",
    )(gate_pre, up_pre, out_grad, old_weight, old_first, old_second)
    new_weight, new_first, new_second = adamw(
        weight.astype(F32), moments[0].astype(F32), moments[1].astype(F32), grad.astype(F32)
    )
    return (new_weight, new_first, new_second, gg, gu)


def solution(mesh):
    placed = (
        P("dp", "tensor"),
        P("dp", "tensor"),
        P("dp", None),
        P(("dp", "tensor"), None),
        P(("dp", "tensor"), None),
        P(("dp", "tensor"), None),
    )
    return jax.shard_map(
        body,
        mesh=mesh,
        in_specs=placed,
        out_specs=(
            P("tensor", "dp"),
            P("tensor", "dp"),
            P("tensor", "dp"),
            P("dp", "tensor"),
            P("dp", "tensor"),
        ),
        check_vma=False,
    )
```
